512 devices in a mesh: gx: 8 (over x, core), gy: 8 (over y), gz: 8 (over z).
Axes of the slice: x: 4, y: 8, z: 8, core: 2. Of those that a mesh axis runs over, the one named last changes fastest.
Arguments:
- populations: float32 [19, 32, 128, 1024], P(None, 'gx', 'gy', 'gz'), may hold values from 0.5 to 2
- solid_mask: int32 [32, 128, 1024], P('gx', 'gy', 'gz'), may hold values 0 or 1
- displacement: float32 [3, 524288], P(None, ('gx', 'gy', 'gz')), may hold values from -2 to 2
- stiffness: float32 [524288], P(('gx', 'gy', 'gz')), may hold values from 0.5 to 5
- neighbours: int32 [6, 524288], P(None, ('gx', 'gy', 'gz')), may hold values from 0 to 1023
- owners: int32 [524288, 1], P(('gx', 'gy', 'gz')), may hold values from 0 to 63; in each aligned block of 1024 rows (0 to 1023, 1024 to 2047, ...) at most 32 rows name the same one
- stencil_base: int32 [524288], P(('gx', 'gy', 'gz')), may hold values from 0 to 1660, as said below
- stencil_weights: float32 [12, 524288], P(None, ('gx', 'gy', 'gz')), may hold values from 0.1 to 0.6
Outputs:
- new_populations: float32 [19, 32, 128, 1024], P(None, 'gx', 'gy', 'gz')
- body_force: float32 [3, 32, 128, 1024], P(None, 'gx', 'gy', 'gz')
The draws below stay inside these ranges and needn't reach their ends.
Inputs may be any that keep to these rules, and one draw needn't show every extreme that they name: `owners`: among the 1024 vertices of one device at most 32 name one brick, a bound that some block reaches. `stencil_base`: each stencil lies wholly inside its owner brick: bx <= 0, by <= 12, bz <= 124.
All inputs are finite; a program needn't handle non-finite values. No bound on the sum of `solid_mask` on one device may be relied on, other than what follows from the above.
Results may differ from the reference program's by a relative error of at most 0.0003.
Values sent between devices are 32-bit elements; how exact they have to be, the bound alone decides.
A program may use at most 64 MiB of HBM per device.

```python
import math
import jax
import jax.numpy as jnp
import numpy as np
from jax import lax

BX = 4
BY = 16
BZ = 128
V_DEV = 1024
NX = 32
NY = 128
NZ = 1024
VERTICES = 524288
CAP = 32
N_GY = 8
N_GZ = 8


def draw_stencil_base(key, part):
    key = jax.random.fold_in(key, 7)
    key_x, key_y, key_z = jax.random.split(key, 3)
    corner_x = jax.random.randint(key_x, (VERTICES,), 0, BX - 3)
    corner_y = jax.random.randint(key_y, (VERTICES,), 0, BY - 3)
    corner_z = jax.random.randint(key_z, (VERTICES,), 0, BZ - 3)
    flat = (corner_x * BY + corner_y) * BZ + corner_z
    flat = flat.at[0].set(0)
    flat = flat.at[VERTICES - 1].set(((BX - 4) * BY + BY - 4) * BZ + BZ - 4)
    return flat.astype(jnp.int32)


def set_ends(result, own_key, low, largest):
    spot = [jax.random.randint(jax.random.fold_in(own_key, axis), (), 0, length) for axis, length in enumerate(result.shape)]
    longest = result.shape.index(max(result.shape))
    beside = spot[:longest] + [(spot[longest] + 1) % result.shape[longest]] + spot[longest + 1:]
    return result.at[tuple(spot)].set(low).at[tuple(beside)].set(largest)


def block_scale(own_key, shape, cuts, smallest, largest):
    def one(axis_at, shards_of):
        steps = jax.random.uniform(jax.random.fold_in(jax.random.fold_in(own_key, 6), axis_at), (shards_of,), jnp.float32, smallest / len(cuts), largest / len(cuts))
        return jnp.repeat(jnp.exp(steps), shape[axis_at] // shards_of).reshape((-1,) + (1,) * (len(shape) - axis_at - 1))

    gain = one(*cuts[0])
    for cut in cuts[1:]:
        gain = gain * one(*cut)
    return gain


def routed_block(own_key, own, number, rows, amount, top, bound, skew):
    order = jax.random.permutation(own_key, amount)
    heavy_load, ordinary = portions_of(amount, rows * top, bound, skew, True), portions_of(amount, rows * top, bound, skew, False)
    places = jnp.arange(amount)

    def named(tallies, turn):
        used = int((tallies > 0).sum())
        fixed = max(1, used // 4)
        passed = fixed + (places - fixed + turn * (used - fixed)) % max(1, amount - fixed)
        return jnp.zeros((amount,), jnp.int32).at[order[jnp.where(places < fixed, places, passed)]].set(jnp.asarray(tallies, jnp.int32))

    tallies = jnp.where(number % 4 == 0, named(heavy_load, number // 4), named(ordinary, number - number // 4 - 1))
    mixed = jax.random.permutation(jax.random.fold_in(own, 3), amount)
    source_of, receiver = mixed[0:amount // 2 * 2:2], mixed[1:amount // 2 * 2:2]
    room = jnp.minimum(tallies[source_of] - 1, bound - tallies[receiver]) // 2
    room = jnp.where((source_of == order[0]) | (receiver == order[0]) | (tallies[receiver] == 0), 0, jnp.maximum(room, 0))
    passed = jax.random.randint(jax.random.fold_in(own, 4), (amount // 2,), 0, 1 << 20) % (room + 1)
    tallies = tallies.at[source_of].add(-passed).at[receiver].add(passed)
    labels = jnp.searchsorted(jnp.cumsum(tallies), jnp.arange(rows * top), side="right").astype(jnp.int32)
    listing = labels.reshape(top, rows).T
    listing = listing[jax.random.permutation(jax.random.fold_in(own, 1), rows)]
    turn = jax.random.randint(jax.random.fold_in(own, 2), (rows, 1), 0, top)
    return jnp.take_along_axis(listing, (jnp.arange(top)[None, :] + turn) % top, axis=1)


def portions_of(number_of, total, reach, skew, full):
    portions = [(1 << 20) // math.isqrt(rank ** skew) + 1 for rank in range(1, number_of + 1)]
    largest = reach if full else min(reach, max(-(-total // number_of), total * portions[0] // sum(portions)))
    least = 1 if total - largest >= number_of - 1 else 0
    given, rest = [largest] + [least] * (number_of - 1), total - largest - least * (number_of - 1)
    while rest > 0:
        movable = [i for i in range(1, number_of) if given[i] < largest] or [i for i in range(1, number_of) if given[i] < reach]
        whole, budget = sum([portions[i] for i in movable]), rest
        for i in movable:
            extra = min(reach - given[i], max(1, budget * portions[i] // whole), rest)
            given[i] = given[i] + extra
            rest = rest - extra
    return np.array(given)


def normal_values(own_key, shape, scale, limit, pieces=(), held_as=jnp.bfloat16):
    values = jax.random.normal(own_key, shape, jnp.float32) * scale
    if len(pieces) > 0:
        values = block_scale(own_key, shape, pieces, -0.22, 0.18) * values
    return jnp.clip(values, min=-limit, max=limit).astype(held_as)


def setup_inputs(seed: int = 0) -> dict:
    key_list = jax.random.split(jax.random.key(seed), 9)
    populations = jnp.clip(jnp.exp(math.log(2.0) - 1.3862944 * jax.random.uniform(key_list[0], (19, NX, NY, NZ), jnp.float32) ** block_scale(key_list[0], (19, NX, NY, NZ), ((1, 8), (2, 8), (3, 8)), -0.2, 0.2)), 0.5, 2.0)
    solid_mask = set_ends((jax.random.randint(key_list[1], (NX, NY, NZ), 0, 8) < 1).astype(jnp.int32), jax.random.fold_in(key_list[1], 1), 0, 1)
    displacement = normal_values(key_list[2], (3, VERTICES), 0.3, 2.0, ((1, 512),), jnp.float32)
    stiffness = jnp.clip(jnp.exp(math.log(5.0) - 2.3025851 * jax.random.uniform(key_list[3], (VERTICES,), jnp.float32) ** block_scale(key_list[3], (VERTICES,), ((0, 512),), -0.2, 0.2)), 0.5, 5.0)
    neighbours = set_ends(jax.random.randint(key_list[4], (6, VERTICES), 0, V_DEV), jax.random.fold_in(key_list[4], 1), 0, V_DEV - 1).astype(jnp.int32)
    owners_keys = jax.random.split(jax.random.fold_in(key_list[5], 1), VERTICES // V_DEV)
    owners_turns = jax.random.permutation(jax.random.fold_in(key_list[5], 3), VERTICES // V_DEV)
    owners = jax.vmap(lambda own, number: routed_block(jax.random.fold_in(key_list[5], 2), own, number, V_DEV, N_GY * N_GZ, 1, CAP, 2))(owners_keys, owners_turns).reshape((VERTICES, 1))
    stencil_base = draw_stencil_base(jax.random.fold_in(key_list[8], 71), 0)
    stencil_weights = jnp.clip(0.1 + 0.5 * jax.random.uniform(key_list[7], (12, VERTICES), jnp.float32) ** block_scale(key_list[7], (12, VERTICES), ((1, 512),), -0.2, 0.2), 0.1, 0.6)
    return dict(populations=populations, solid_mask=solid_mask, displacement=displacement, stiffness=stiffness, neighbours=neighbours, owners=owners, stencil_base=stencil_base, stencil_weights=stencil_weights)


velocity_x = np.array([0, 1, -1, 0, 0, 0, 0, 1, -1, 1, -1, 1, -1, 1, -1, 0, 0, 0, 0], dtype=np.float32)
velocity_y = np.array([0, 0, 0, 1, -1, 0, 0, 1, -1, -1, 1, 0, 0, 0, 0, 1, -1, 1, -1], dtype=np.float32)
velocity_z = np.array([0, 0, 0, 0, 0, 1, -1, 0, 0, 0, 0, 1, -1, -1, 1, 1, -1, -1, 1], dtype=np.float32)
lattice_weight = np.array([1.0 / 3.0] + [1.0 / 18.0] * 6 + [1.0 / 36.0] * 12, dtype=np.float32)
opposite = np.array([0, 2, 1, 4, 3, 6, 5, 8, 7, 10, 9, 12, 11, 14, 13, 16, 15, 18, 17])
relax_time = 0.8


def collide(shifted, force, solid):
    shape = (19,) + (1,) * (shifted.ndim - 1)
    dir_x = velocity_x.reshape(shape)
    dir_y = velocity_y.reshape(shape)
    dir_z = velocity_z.reshape(shape)
    weight = lattice_weight.reshape(shape)
    density = jnp.sum(shifted, axis=0)
    flow_x = (jnp.sum(dir_x * shifted, axis=0) + 0.5 * force[0]) / density
    flow_y = (jnp.sum(dir_y * shifted, axis=0) + 0.5 * force[1]) / density
    flow_z = (jnp.sum(dir_z * shifted, axis=0) + 0.5 * force[2]) / density
    along = dir_x * flow_x + dir_y * flow_y + dir_z * flow_z
    speed_sq = flow_x * flow_x + flow_y * flow_y + flow_z * flow_z
    equilib = weight * density * (1.0 + 3.0 * along + 4.5 * along * along - 1.5 * speed_sq)
    push = dir_x * force[0] + dir_y * force[1] + dir_z * force[2]
    work = flow_x * force[0] + flow_y * force[1] + flow_z * force[2]
    source = (1.0 - 0.5 / relax_time) * weight * (3.0 * (push - work) + 9.0 * along * push)
    fluid = shifted - (shifted - equilib) / relax_time + source
    return jnp.where(solid[None] == 1, shifted[opposite], fluid)


def reference(populations, solid_mask, displacement, stiffness, neighbours, owners, stencil_base, stencil_weights):
    count = displacement.shape[1]
    block_id = jnp.arange(count, dtype=jnp.int32) // V_DEV
    global_nbr = neighbours + (block_id * V_DEV)[None, :]
    vertex_force = stiffness[None, :] * (jnp.sum(displacement[:, global_nbr], axis=1) - 6.0 * displacement)
    group = N_GY * N_GZ
    owner = owners[:, 0]
    anchor_x = (block_id // group) * BX + stencil_base // (BY * BZ)
    anchor_y = (owner // N_GZ) * BY + (stencil_base // BZ) % BY
    anchor_z = (owner % N_GZ) * BZ + stencil_base % BZ

    def add_offset(offset, field):
        step_x = offset // 16
        step_y = (offset // 4) % 4
        step_z = offset % 4
        wgt_x = lax.dynamic_index_in_dim(stencil_weights, step_x, 0, keepdims=False)
        wgt_y = lax.dynamic_index_in_dim(stencil_weights, 4 + step_y, 0, keepdims=False)
        wgt_z = lax.dynamic_index_in_dim(stencil_weights, 8 + step_z, 0, keepdims=False)
        place = ((anchor_x + step_x) * NY + anchor_y + step_y) * NZ + anchor_z + step_z
        value = vertex_force * wgt_x[None, :] * wgt_y[None, :] * wgt_z[None, :]
        return field.at[:, place].add(value)

    flat = lax.fori_loop(0, 64, add_offset, jnp.zeros((3, NX * NY * NZ), jnp.float32))
    body_force = flat.reshape(3, NX, NY, NZ)
    rows = []
    for index in range(19):
        shift = (int(velocity_x[index]), int(velocity_y[index]), int(velocity_z[index]))
        rows.append(jnp.roll(populations[index], shift, axis=(0, 1, 2)))
    shifted = jnp.stack(rows)
    slabs = lax.map(lambda items: collide(items[0], items[1], items[2]),
                    (jnp.moveaxis(shifted, 1, 0), jnp.moveaxis(body_force, 1, 0), solid_mask))
    new_populations = jnp.moveaxis(slabs, 0, 1)
    return new_populations, body_force
```

```python
import functools

import jax
import jax.numpy as jnp
import numpy as np
from jax import lax
from jax.experimental import pallas as pl
from jax.experimental.pallas import tpu as pltpu
from jax.sharding import PartitionSpec as P

MESH = pl.DeviceIdType.MESH
F32 = jnp.float32
BF16 = jnp.bfloat16
I32 = jnp.int32

VEL = (
    (0, 0, 0),
    (1, 0, 0), (-1, 0, 0), (0, 1, 0), (0, -1, 0), (0, 0, 1), (0, 0, -1),
    (1, 1, 0), (-1, -1, 0), (1, -1, 0), (-1, 1, 0),
    (1, 0, 1), (-1, 0, -1), (1, 0, -1), (-1, 0, 1),
    (0, 1, 1), (0, -1, -1), (0, 1, -1), (0, -1, 1),
)
SX, SY, SZ = 4, 16, 128
N_GY = N_GZ = 8
GROUP = N_GY * N_GZ
FACE = tuple(
    tuple(tuple(i for i in range(19) if VEL[i][axis] == sign) for sign in (1, -1))
    for axis in range(3)
)
EDGE_XY = (7, 8, 9, 10)
EDGE_XZ = (11, 12, 13, 14)
EDGE_YZ = (15, 16, 17, 18)


def side(sign):
    return 0 if sign > 0 else 1


def face_slot(axis, i):
    s = side(VEL[i][axis])
    return s, FACE[axis][s].index(i)


def bf(x):
    return x.astype(BF16)


def dot_nt(a, b):
    return lax.dot_general(a, b, (((1,), (1,)), ((), ())), preferred_element_type=F32)


def lane_gather(table, index):
    return jnp.take_along_axis(table, index, axis=1, mode="promise_in_bounds")


def pack_faces(pop, hx, hy, hz):
    for s in range(2):
        for k, i in enumerate(FACE[0][s]):
            hx[s, k] = pop[i, 3 if s == 0 else 0]
        row = 15 if s == 0 else 0
        for k, i in enumerate(FACE[1][s]):
            for x in range(SX):
                hy[s, k, x : x + 1, :] = pop[i, x, row : row + 1, :]
        lane = lax.broadcasted_iota(I32, (8, 128), 1)
        edge = 127 if s == 0 else 0
        packed = jnp.zeros((8, 128), F32)
        for k, i in enumerate(FACE[2][s]):
            for x in range(SX):
                for half in range(2):
                    place = 16 * (2 * x + half) + k
                    rolled = pltpu.roll(pop[i, x, 8 * half : 8 * half + 8, :], (place - edge) % 128, 1)
                    packed = jnp.where(lane == place, rolled, packed)
        hz[s] = packed


def pack_vertices(disp, stiff, nbr, owner, base, weights, send, pay):
    lane = lax.broadcasted_iota(I32, (1, 128), 1)
    for v in range(8):
        here = pl.ds(128 * v, 128)
        index = nbr[:, here]
        low, high = index & 127, index >> 7
        for c in range(3):
            total = jnp.zeros((6, 128), F32)
            for k in range(8):
                table = jnp.broadcast_to(disp[c : c + 1, 128 * k : 128 * k + 128], (6, 128))
                total = jnp.where(high == k, lane_gather(table, low), total)
            summed = jnp.sum(total, axis=0, keepdims=True)
            pay[c : c + 1, here] = stiff[:, here] * (summed - 6.0 * disp[c : c + 1, here])
        pay[3:4, here] = base[:, here].astype(F32)
    own = owner[...]
    group_ids = lax.broadcasted_iota(I32, (GROUP, 128), 0)
    member = [jnp.where(own[:, 128 * v : 128 * v + 128] == group_ids, 1.0, 0.0) for v in range(8)]
    before = [jnp.zeros((GROUP, 128), F32)]
    for v in range(7):
        before.append(before[v] + member[v])
    stacked = jnp.concatenate(
        [jnp.concatenate([bf(member[v]), bf(before[v])], axis=1) for v in range(8)], axis=0
    )
    rows = lax.broadcasted_iota(I32, (256, 128), 0)
    cols = lax.broadcasted_iota(I32, (256, 128), 1)
    upto = bf(jnp.where((rows <= cols) | (rows >= 128), 1.0, 0.0))
    running = jnp.dot(stacked, upto, preferred_element_type=F32)
    quad_ids = lax.broadcasted_iota(I32, (GROUP // 4, 128), 0)
    slot_ids = lax.broadcasted_iota(I32, (128, 128), 0)
    lefts, rights = [], []
    for v in range(8):
        rank = jnp.sum(member[v] * running[GROUP * v : GROUP * v + GROUP], axis=0, keepdims=True) - 1.0
        own_v = own[:, 128 * v : 128 * v + 128]
        slot = (own_v & 3) * 32 + rank.astype(I32)
        quad = (own_v >> 2) == quad_ids
        lefts.append(
            jnp.concatenate(
                [
                    bf(jnp.where(quad, lane.astype(F32), 0.0)),
                    bf(jnp.where(quad, float(v + 1), 0.0)),
                ],
                axis=0,
            )
        )
        rights.append(bf(jnp.where(slot == slot_ids, 1.0, 0.0)))
    found = dot_nt(jnp.concatenate(lefts, axis=1), jnp.concatenate(rights, axis=1))
    found = found.astype(I32)
    low, high = found[0:16], found[16:32] - 1
    lows = [low] + [pltpu.roll(low, 32 * j, 1) for j in range(1, 4)]
    highs = [high] + [pltpu.roll(high, 32 * j, 1) for j in range(1, 4)]
    lane_quad = lax.broadcasted_iota(I32, (16, 128), 1) >> 5
    for r in range(4):
        picked = []
        for pl_ in range(4):
            p = 4 * r + pl_
            got = jnp.zeros((16, 128), F32)
            for k in range(8):
                if p < 4:
                    row = pay[p : p + 1, 128 * k : 128 * k + 128]
                else:
                    row = weights[p - 4 : p - 3, 128 * k : 128 * k + 128]
                table = jnp.broadcast_to(row, (16, 128))
                got = jnp.where(highs[pl_] == k, lane_gather(table, lows[pl_]), got)
            picked.append(got)
        for q in range(4):
            mixed = picked[0]
            for pl_ in range(1, 4):
                mixed = jnp.where(lane_quad == (q + pl_) % 4, picked[pl_], mixed)
            if q:
                mixed = pltpu.roll(mixed, 128 - 32 * q, 1)
            send[pl.ds(4 * q + r, 16, stride=16), :] = mixed


def prep_kernel(pop, disp, stiff, nbr, owner, base, weights, send, hx, hy, hz, pay):
    pack_faces(pop, hx, hy, hz)
    pack_vertices(disp, stiff, nbr, owner, base, weights, send, pay)


def halo_messages(hx, hy, hz, got_hx, got_hy, got_hz, got_xy, got_xz, got_yz):
    messages = []
    for s, sign in enumerate((1, -1)):
        messages.append(((sign, 0, 0), hx.at[s], got_hx.at[s]))
        messages.append(((0, sign, 0), hy.at[s], got_hy.at[s]))
        messages.append(((0, 0, sign), hz.at[s], got_hz.at[s]))
    for n, i in enumerate(EDGE_XY):
        s, k = face_slot(1, i)
        messages.append((VEL[i], hy.at[s, k], got_xy.at[n]))
    for n, i in enumerate(EDGE_XZ):
        s, k = face_slot(0, i)
        messages.append((VEL[i], hx.at[s, k], got_xz.at[n]))
    for n, i in enumerate(EDGE_YZ):
        s, k = face_slot(1, i)
        messages.append((VEL[i], hy.at[s, k], got_yz.at[n]))
    return messages


def exchange_kernel(
    send, hx, hy, hz, got, got_hx, got_hy, got_hz, got_xy, got_xz, got_yz,
    send_sem, recv_sem, halo_send, halo_recv, own_sem,
):
    gx, gy, gz = lax.axis_index("gx"), lax.axis_index("gy"), lax.axis_index("gz")
    me = gy * N_GZ + gz

    def device(dx, dy, dz):
        return {
            "gx": lax.rem(gx + dx + 8, 8),
            "gy": lax.rem(gy + dy + N_GY, N_GY),
            "gz": lax.rem(gz + dz + N_GZ, N_GZ),
        }

    messages = halo_messages(hx, hy, hz, got_hx, got_hy, got_hz, got_xy, got_xz, got_yz)
    barrier = pltpu.get_barrier_semaphore()
    outside = [m[0] for m in messages if m[0][0] != 0]
    for step in outside:
        pl.semaphore_signal(barrier, inc=1, device_id=device(*step), device_id_type=MESH)

    def greet(t, carry):
        pl.semaphore_signal(
            barrier, inc=1, device_id=device(0, t // N_GZ, lax.rem(t, N_GZ)), device_id_type=MESH
        )
        return carry

    lax.fori_loop(1, GROUP, greet, 0)
    pl.semaphore_wait(barrier, GROUP - 1 + len(outside))

    own = pltpu.make_async_copy(send.at[me], got.at[me], own_sem)
    own.start()
    halos = []
    for n, (step, src, dst) in enumerate(messages):
        copy = pltpu.make_async_remote_copy(
            src_ref=src, dst_ref=dst, send_sem=halo_send.at[n], recv_sem=halo_recv.at[n],
            device_id=device(*step), device_id_type=MESH,
        )
        copy.start()
        halos.append(copy)

    def vertex_copy(t, outgoing):
        dy, dz = t // N_GZ, lax.rem(t, N_GZ)
        if outgoing:
            there = device(0, dy, dz)
            index, slot = there["gy"] * N_GZ + there["gz"], me
        else:
            there = device(0, N_GY - dy, N_GZ - dz)
            index = slot = there["gy"] * N_GZ + there["gz"]
        return pltpu.make_async_remote_copy(
            src_ref=send.at[index], dst_ref=got.at[slot],
            send_sem=send_sem.at[t], recv_sem=recv_sem.at[t],
            device_id=there, device_id_type=MESH,
        )

    def start(t, carry):
        vertex_copy(t, True).start()
        return carry

    def finish_in(t, carry):
        vertex_copy(t, False).wait_recv()
        return carry

    def finish_out(t, carry):
        vertex_copy(t, True).wait_send()
        return carry

    lax.fori_loop(1, GROUP, start, 0)
    for copy in halos:
        copy.wait()
    own.wait()
    lax.fori_loop(1, GROUP, finish_in, 0)
    lax.fori_loop(1, GROUP, finish_out, 0)


def spread(got, force, quads, left, table):
    lane_quad = lax.broadcasted_iota(I32, (16, 128), 1) >> 5
    for r in range(4):
        skewed = []
        for j in range(4):
            block = got[pl.ds(4 * j + r, 16, stride=16), :]
            skewed.append(pltpu.roll(block, 32 * j, 1) if j else block)
        for pl_ in range(4):
            mixed = skewed[0]
            for j in range(1, 4):
                mixed = jnp.where(lane_quad == (pl_ + j) % 4, skewed[j], mixed)
            if pl_:
                mixed = pltpu.roll(mixed, 128 - 32 * pl_, 1)
            quads[4 * r + pl_] = mixed
    iota_y = lax.broadcasted_iota(I32, (SY, 128), 0).astype(F32)
    iota_z = lax.broadcasted_iota(I32, (SZ, 128), 0).astype(F32)
    for g in range(16):
        here = pl.ds(128 * g, 128)

        def row(p):
            return quads[p, g : g + 1, :]

        corner = row(3).astype(I32)
        corner_y, corner_z = (corner >> 7).astype(F32), (corner & 127).astype(F32)
        off_y = iota_y - corner_y
        off_z = iota_z - corner_z
        table_y = jnp.zeros((SY, 128), F32)
        for j in range(4):
            table_y = jnp.where(off_y == float(j), row(8 + j), table_y)
        high = jnp.zeros((SZ, 128), F32)
        low = jnp.zeros((SZ, 128), F32)
        for k in range(4):
            weight = row(12 + k)
            weight_high = bf(weight).astype(F32)
            hit = off_z == float(k)
            high = jnp.where(hit, weight_high, high)
            low = jnp.where(hit, weight - weight_high, low)
        table[0:SZ, here] = bf(high)
        table[SZ : 2 * SZ, here] = bf(low)
        for c in range(3):
            for x in range(SX):
                value = (row(c) * row(4 + x)) * table_y
                value_high = bf(value)
                place = (c * SX + x) * SY
                left[place : place + SY, here] = value_high
                left[192 + place : 192 + place + SY, here] = bf(value - value_high.astype(F32))
    out = dot_nt(left[...], table[...])
    total = out[0:192, 0:SZ] + (out[192:384, 0:SZ] + out[0:192, SZ : 2 * SZ])
    for c in range(3):
        for x in range(SX):
            place = (c * SX + x) * SY
            force[c, x] = total[place : place + SY]


def moved(pop, halos, i, x, masks):
    hx, hy, hz, exy, exz, eyz = halos
    cx, cy, cz = VEL[i]
    source = x - cx
    inside = 0 <= source < SX
    if inside:
        cells = pop[i, source]
    else:
        cells = hx[face_slot(0, i)]
    if cz:
        cells = pltpu.roll(cells, cz % 128, 1)
        s, k = face_slot(2, i)
        edge = 0 if cz > 0 else 127
        if inside:
            packed = hz[s]
            column = jnp.concatenate(
                [pltpu.roll(packed, (edge - 16 * (2 * source + half) - k) % 128, 1) for half in range(2)],
                axis=0,
            )
        else:
            column = pltpu.roll(exz[EDGE_XZ.index(i)], cz % 128, 1)
        cells = jnp.where(masks["z", cz], column, cells)
    if cy:
        cells = pltpu.roll(cells, cy % 16, 0)
        if inside:
            line = hy[face_slot(1, i)]
            if cz:
                line = pltpu.roll(line, cz % 128, 1)
                beyond = pltpu.roll(eyz[EDGE_YZ.index(i)], cz % 128, 1)
                line = jnp.where(masks["z4", cz], beyond, line)
        else:
            line = exy[EDGE_XY.index(i)]
        line = line[source % SX : source % SX + 1]
        cells = jnp.where(masks["y", cy], jnp.broadcast_to(line, (SY, SZ)), cells)
    return cells


def collide(pop, solid, force, halos, new):
    lane = lax.broadcasted_iota(I32, (SY, SZ), 1)
    line = lax.broadcasted_iota(I32, (SY, SZ), 0)
    lane4 = lax.broadcasted_iota(I32, (SX, SZ), 1)
    masks = {
        ("z", 1): lane == 0, ("z", -1): lane == SZ - 1,
        ("z4", 1): lane4 == 0, ("z4", -1): lane4 == SZ - 1,
        ("y", 1): line == 0, ("y", -1): line == SY - 1,
    }
    for x in range(SX):
        s = [moved(pop, halos, i, x, masks) for i in range(19)]
        density = s[0]
        momentum = [None, None, None]
        for i in range(1, 19, 2):
            density = density + (s[i] + s[i + 1])
            gap = s[i] - s[i + 1]
            for axis in range(3):
                c = VEL[i][axis]
                if c:
                    old = momentum[axis]
                    if old is None:
                        momentum[axis] = gap
                    else:
                        momentum[axis] = old + gap if c > 0 else old - gap
        push = [force[c, x] for c in range(3)]
        inverse = 1.0 / density
        flow = [(momentum[a] + 0.5 * push[a]) * inverse for a in range(3)]
        speed = flow[0] * flow[0] + flow[1] * flow[1] + flow[2] * flow[2]
        work = flow[0] * push[0] + flow[1] * push[1] + flow[2] * push[2]
        wall = solid[x] == 1
        common = density * (1.25 - 1.875 * speed) - 1.125 * work
        square = 5.625 * density
        linear = 3.75 * density
        new[0, x] = jnp.where(wall, s[0], (1.0 / 3.0) * common - 0.25 * s[0])
        for i in range(1, 19, 2):
            weight = 1.0 / 18.0 if i < 7 else 1.0 / 36.0
            a = b = None
            for axis in range(3):
                c = VEL[i][axis]
                if c:
                    if a is None:
                        a, b = flow[axis], push[axis]
                    elif c > 0:
                        a, b = a + flow[axis], b + push[axis]
                    else:
                        a, b = a - flow[axis], b - push[axis]
            even = weight * (common + a * (square * a + 3.375 * b))
            odd = weight * (linear * a + 1.125 * b)
            new[i, x] = jnp.where(wall, s[i + 1], (even + odd) - 0.25 * s[i])
            new[i + 1, x] = jnp.where(wall, s[i], (even - odd) - 0.25 * s[i + 1])


def lattice_kernel(
    pop, solid, got, hx, hy, hz, exy, exz, eyz, new, force, quads, left, table
):
    spread(got, force, quads, left, table)
    collide(pop, solid, force, (hx, hy, hz, exy, exz, eyz), new)


def whole(count):
    return [pl.BlockSpec(memory_space=pltpu.VMEM)] * count


def local(populations, solid_mask, displacement, stiffness, neighbours, owners, stencil_base, stencil_weights):
    def f32(*shape):
        return jax.ShapeDtypeStruct(shape, F32)

    halo_shapes = (f32(2, 5, SY, SZ), f32(2, 5, SX, SZ), f32(2, 8, 128))
    send, hx, hy, hz = pl.pallas_call(
        prep_kernel,
        out_shape=(f32(256, 128),) + halo_shapes,
        in_specs=whole(7),
        out_specs=tuple(whole(4)),
        scratch_shapes=[pltpu.VMEM((4, 1024), F32)],
        name="prepare",
    )(
        populations, displacement, stiffness.reshape(1, 1024), neighbours,
        owners.reshape(1, 1024), stencil_base.reshape(1, 1024), stencil_weights,
    )
    received = pl.pallas_call(
        exchange_kernel,
        out_shape=(f32(GROUP, 4, 128),) + halo_shapes + (f32(4, SX, SZ), f32(4, SY, SZ), f32(4, SX, SZ)),
        in_specs=whole(4),
        out_specs=tuple(whole(7)),
        scratch_shapes=[
            pltpu.SemaphoreType.DMA((GROUP,)),
            pltpu.SemaphoreType.DMA((GROUP,)),
            pltpu.SemaphoreType.DMA((18,)),
            pltpu.SemaphoreType.DMA((18,)),
            pltpu.SemaphoreType.DMA,
        ],
        compiler_params=pltpu.CompilerParams(collective_id=0, has_side_effects=True),
        name="exchange",
    )(send.reshape(GROUP, 4, 128), hx, hy, hz)
    got, halos = received[0], received[1:]
    return tuple(
        pl.pallas_call(
            lattice_kernel,
            out_shape=(f32(19, SX, SY, SZ), f32(3, SX, SY, SZ)),
            in_specs=whole(9),
            out_specs=tuple(whole(2)),
            scratch_shapes=[
                pltpu.VMEM((16, 16, 128), F32),
                pltpu.VMEM((384, 2048), BF16),
                pltpu.VMEM((256, 2048), BF16),
            ],
            compiler_params=pltpu.CompilerParams(vmem_limit_bytes=24 * 1024 * 1024),
            name="lattice",
        )(populations, solid_mask, got.reshape(256, 128), *halos)
    )


def solution(mesh):
    placed = (
        P(None, "gx", "gy", "gz"),
        P("gx", "gy", "gz"),
        P(None, ("gx", "gy", "gz")),
        P(("gx", "gy", "gz")),
        P(None, ("gx", "gy", "gz")),
        P(("gx", "gy", "gz"), None),
        P(("gx", "gy", "gz")),
        P(None, ("gx", "gy", "gz")),
    )
    return jax.shard_map(
        local,
        mesh=mesh,
        in_specs=placed,
        out_specs=(P(None, "gx", "gy", "gz"), P(None, "gx", "gy", "gz")),
        check_vma=False,
    )
```

```python
import functools

import jax
import jax.numpy as jnp
import numpy as np
from jax import lax
from jax.experimental import pallas as pl
from jax.experimental.pallas import tpu as pltpu
from jax.sharding import PartitionSpec as P

MESH = pl.DeviceIdType.MESH
F32 = jnp.float32
BF16 = jnp.bfloat16
I32 = jnp.int32

VEL = (
    (0, 0, 0),
    (1, 0, 0), (-1, 0, 0), (0, 1, 0), (0, -1, 0), (0, 0, 1), (0, 0, -1),
    (1, 1, 0), (-1, -1, 0), (1, -1, 0), (-1, 1, 0),
    (1, 0, 1), (-1, 0, -1), (1, 0, -1), (-1, 0, 1),
    (0, 1, 1), (0, -1, -1), (0, 1, -1), (0, -1, 1),
)
SX, SY, SZ = 4, 16, 128
N_GY = N_GZ = 8
GROUP = N_GY * N_GZ
FACE = tuple(
    tuple(tuple(i for i in range(19) if VEL[i][axis] == sign) for sign in (1, -1))
    for axis in range(3)
)
EDGE_XY = (7, 8, 9, 10)
EDGE_XZ = (11, 12, 13, 14)
EDGE_YZ = (15, 16, 17, 18)


def side(sign):
    return 0 if sign > 0 else 1


def face_slot(axis, i):
    s = side(VEL[i][axis])
    return s, FACE[axis][s].index(i)


def bf(x):
    return x.astype(BF16)


def dot_nt(a, b):
    return lax.dot_general(a, b, (((1,), (1,)), ((), ())), preferred_element_type=F32)


def lane_gather(table, index):
    return jnp.take_along_axis(table, index, axis=1, mode="promise_in_bounds")


def pack_faces(pop, hx, hy, hz):
    for s in range(2):
        for k, i in enumerate(FACE[0][s]):
            hx[s, k] = pop[i, 3 if s == 0 else 0]
        row = 15 if s == 0 else 0
        for k, i in enumerate(FACE[1][s]):
            for x in range(SX):
                hy[s, k, x : x + 1, :] = pop[i, x, row : row + 1, :]
        lane = lax.broadcasted_iota(I32, (8, 128), 1)
        edge = 127 if s == 0 else 0
        packed = jnp.zeros((8, 128), F32)
        for k, i in enumerate(FACE[2][s]):
            for x in range(SX):
                for half in range(2):
                    place = 16 * (2 * x + half) + k
                    rolled = pltpu.roll(pop[i, x, 8 * half : 8 * half + 8, :], (place - edge) % 128, 1)
                    packed = jnp.where(lane == place, rolled, packed)
        hz[s] = packed


def pack_vertices(disp, stiff, nbr, owner, base, weights, send, pay):
    lane = lax.broadcasted_iota(I32, (1, 128), 1)
    own = owner[...]
    group_ids = lax.broadcasted_iota(I32, (GROUP, 128), 0)
    member = [jnp.where(own[:, 128 * v : 128 * v + 128] == group_ids, 1.0, 0.0) for v in range(8)]
    before = [jnp.zeros((GROUP, 128), F32)]
    for v in range(7):
        before.append(before[v] + member[v])
    stacked = jnp.concatenate(
        [jnp.concatenate([bf(member[v]), bf(before[v])], axis=1) for v in range(8)], axis=0
    )
    rows = lax.broadcasted_iota(I32, (256, 128), 0)
    cols = lax.broadcasted_iota(I32, (256, 128), 1)
    upto = bf(jnp.where((rows <= cols) | (rows >= 128), 1.0, 0.0))
    running = jnp.dot(stacked, upto, preferred_element_type=F32)
    for v in range(8):
        here = slice(128 * v, 128 * v + 128)
        index = nbr[:, here]
        low, high = index & 127, index >> 7
        for c in range(3):
            total = jnp.zeros((6, 128), F32)
            for k in range(8):
                table = jnp.broadcast_to(disp[c : c + 1, 128 * k : 128 * k + 128], (6, 128))
                total = jnp.where(high == k, lane_gather(table, low), total)
            summed = jnp.sum(total, axis=0, keepdims=True)
            value = stiff[:, here] * (summed - 6.0 * disp[c : c + 1, here])
            pay[c, 0:1, here] = value
            pay[c, 4:5, here] = value
        value = base[:, here].astype(F32)
        pay[3, 0:1, here] = value
        pay[3, 4:5, here] = value
    for l in range(4):
        for i in range(3):
            value = weights[4 * i + l : 4 * i + l + 1, :]
            pay[l, i + 1 : i + 2, :] = value
            pay[l, i + 5 : i + 6, :] = value
    quad_ids = lax.broadcasted_iota(I32, (GROUP // 4, 128), 0)
    slot_ids = lax.broadcasted_iota(I32, (128, 128), 0)
    lefts, rights = [], []
    for v in range(8):
        rank = jnp.sum(member[v] * running[GROUP * v : GROUP * v + GROUP], axis=0, keepdims=True) - 1.0
        own_v = own[:, 128 * v : 128 * v + 128]
        slot = (own_v & 3) * 32 + rank.astype(I32)
        quad = (own_v >> 2) == quad_ids
        lefts.append(
            jnp.concatenate(
                [
                    bf(jnp.where(quad, lane.astype(F32), 0.0)),
                    bf(jnp.where(quad, float(v + 1), 0.0)),
                ],
                axis=0,
            )
        )
        rights.append(bf(jnp.where(slot == slot_ids, 1.0, 0.0)))
    found = dot_nt(jnp.concatenate(lefts, axis=1), jnp.concatenate(rights, axis=1))
    code = (found[0:16] + 128.0 * found[16:32]).astype(I32)
    codes = [code] + [pltpu.roll(code, 32 * j, 1) for j in range(1, 4)]
    lane_quad = lax.broadcasted_iota(I32, (8, 128), 1) >> 5
    for h in range(8):
        picked = []
        for l in range(4):
            pair = jnp.concatenate(
                [jnp.broadcast_to(codes[l][g : g + 1], (4, 128)) for g in (2 * h, 2 * h + 1)], axis=0
            )
            low, high = pair & 127, pair >> 7
            got = jnp.zeros((8, 128), F32)
            for k in range(8):
                got = jnp.where(high == k + 1, lane_gather(pay[l, :, 128 * k : 128 * k + 128], low), got)
            picked.append(got)
        for q in range(4):
            mixed = picked[0]
            for l in range(1, 4):
                mixed = jnp.where(lane_quad == (q + l) % 4, picked[l], mixed)
            if q:
                mixed = pltpu.roll(mixed, 128 - 32 * q, 1)
            send[8 * h + q] = mixed[0:4]
            send[8 * h + 4 + q] = mixed[4:8]


def spread_step(got, sources, quads, left, table):
    lane_quad = lax.broadcasted_iota(I32, (4, 128), 1) >> 5
    iota_y = lax.broadcasted_iota(I32, (SY, 128), 0).astype(F32)
    iota_z = lax.broadcasted_iota(I32, (SZ, 128), 0).astype(F32)
    for n, g in enumerate(sources):
        here = slice(128 * n, 128 * n + 128)
        skewed = [got[4 * g + j] for j in range(4)]
        skewed = [pltpu.roll(skewed[j], 32 * j, 1) if j else skewed[j] for j in range(4)]
        for l in range(4):
            mixed = skewed[0]
            for j in range(1, 4):
                mixed = jnp.where(lane_quad == (l + j) % 4, skewed[j], mixed)
            if l:
                mixed = pltpu.roll(mixed, 128 - 32 * l, 1)
            quads[g, l] = mixed

        def row(p):
            return quads[g, p % 4, p // 4 : p // 4 + 1, :]

        corner = row(3).astype(I32)
        off_y = iota_y - (corner >> 7).astype(F32)
        off_z = iota_z - (corner & 127).astype(F32)
        table_y = jnp.zeros((SY, 128), F32)
        for j in range(4):
            table_y = jnp.where(off_y == float(j), row(8 + j), table_y)
        high = jnp.zeros((SZ, 128), F32)
        low = jnp.zeros((SZ, 128), F32)
        for k in range(4):
            weight = row(12 + k)
            weight_high = bf(weight).astype(F32)
            hit = off_z == float(k)
            high = jnp.where(hit, weight_high, high)
            low = jnp.where(hit, weight - weight_high, low)
        table[0:SZ, here] = bf(high)
        table[SZ : 2 * SZ, here] = bf(low)
        for c in range(3):
            for x in range(SX):
                value = (row(c) * row(4 + x)) * table_y
                value_high = bf(value)
                place = (c * SX + x) * SY
                left[place : place + SY, here] = value_high
                left[192 + place : 192 + place + SY, here] = bf(value - value_high.astype(F32))
    return dot_nt(left[...], table[...])


def moved(pop, halos, i, x, masks):
    hx, hy, hz, exy, exz, eyz = halos
    cx, cy, cz = VEL[i]
    source = x - cx
    inside = 0 <= source < SX
    if inside:
        cells = pop[i, source]
    else:
        cells = hx[face_slot(0, i)]
    if cz:
        cells = pltpu.roll(cells, cz % 128, 1)
        s, k = face_slot(2, i)
        edge = 0 if cz > 0 else 127
        if inside:
            packed = hz[s]
            column = jnp.concatenate(
                [pltpu.roll(packed, (edge - 16 * (2 * source + half) - k) % 128, 1) for half in range(2)],
                axis=0,
            )
        else:
            column = pltpu.roll(exz[EDGE_XZ.index(i)], cz % 128, 1)
        cells = jnp.where(masks["z", cz], column, cells)
    if cy:
        cells = pltpu.roll(cells, cy % 16, 0)
        if inside:
            line = hy[face_slot(1, i)]
            if cz:
                line = pltpu.roll(line, cz % 128, 1)
                beyond = pltpu.roll(eyz[EDGE_YZ.index(i)], cz % 128, 1)
                line = jnp.where(masks["z4", cz], beyond, line)
        else:
            line = exy[EDGE_XY.index(i)]
        line = line[source % SX : source % SX + 1]
        cells = jnp.where(masks["y", cy], jnp.broadcast_to(line, (SY, SZ)), cells)
    return cells


def halo_messages(hx, hy, hz, got_hx, got_hy, got_hz, got_xy, got_xz, got_yz):
    messages = []
    for s, sign in enumerate((1, -1)):
        messages.append(((sign, 0, 0), hx.at[s], got_hx.at[s]))
        messages.append(((0, sign, 0), hy.at[s], got_hy.at[s]))
        messages.append(((0, 0, sign), hz.at[s], got_hz.at[s]))
    for n, i in enumerate(EDGE_XY):
        s, k = face_slot(1, i)
        messages.append((VEL[i], hy.at[s, k], got_xy.at[n]))
    for n, i in enumerate(EDGE_XZ):
        s, k = face_slot(0, i)
        messages.append((VEL[i], hx.at[s, k], got_xz.at[n]))
    for n, i in enumerate(EDGE_YZ):
        s, k = face_slot(1, i)
        messages.append((VEL[i], hy.at[s, k], got_yz.at[n]))
    return messages


def gather_kernel(
    pop_hbm, disp, stiff, nbr, owner, base, weights, shifted, force,
    pop, pay, send, got, hx, hy, hz, got_hx, got_hy, got_hz, got_xy, got_xz, got_yz,
    quads, left, table, total,
    load_sem, send_sem, recv_sem, halo_send, halo_recv, late_sem,
):
    gx, gy, gz = lax.axis_index("gx"), lax.axis_index("gy"), lax.axis_index("gz")
    me = gy * N_GZ + gz
    first = gz < 4

    def place(dx, dy, dz):
        return {
            "gx": lax.rem(gx + dx + 8, 8),
            "gy": lax.rem(gy + dy + N_GY, N_GY),
            "gz": lax.rem(gz + dz + N_GZ, N_GZ),
        }

    def signal(semaphore, device):
        pl.semaphore_signal(semaphore, inc=1, device_id=device, device_id_type=MESH)

    messages = halo_messages(hx, hy, hz, got_hx, got_hy, got_hz, got_xy, got_xz, got_yz)
    barrier = pltpu.get_barrier_semaphore()
    outside = [m[0] for m in messages if m[0][0] != 0]

    @pl.when(first)
    def _():
        for t in range(1, GROUP):
            signal(barrier, place(0, t // N_GZ, t % N_GZ))

    for step in outside:
        signal(barrier, place(*step))
    load = pltpu.make_async_copy(pop_hbm, pop, load_sem)
    load.start()

    pack_vertices(disp, stiff, nbr, owner, base, weights, send, pay)

    @pl.when(first)
    def _():
        pl.semaphore_wait(barrier, 31 + len(outside))

    @pl.when(jnp.logical_not(first))
    def _():
        pl.semaphore_wait(barrier, 32 + len(outside))
        for k in range(8):
            for z in range(4):
                signal(late_sem, {"gx": gx, "gy": lax.rem(gy + k, N_GY), "gz": z})

    def vertex_copy(y, z):
        index = y * N_GZ + z
        return pltpu.make_async_remote_copy(
            src_ref=send.at[index], dst_ref=got.at[me],
            send_sem=send_sem.at[index], recv_sem=recv_sem.at[me],
            device_id={"gx": gx, "gy": y, "gz": z}, device_id_type=MESH,
        )

    def vertex_copies(planes, act):
        for z in planes:
            for k in range(8):
                copy = vertex_copy(lax.rem(gy + k, N_GY), z)
                if k:
                    act(copy)
                else:
                    pl.when(gz != z)(functools.partial(act, copy))

    vertex_copies(range(0, 4), lambda copy: copy.start())
    own = pltpu.make_async_copy(send.at[me], got.at[me], recv_sem.at[me])
    own.start()

    load.wait()
    pack_faces(pop, hx, hy, hz)
    halos = []
    for n, (step, src, dst) in enumerate(messages):
        halos.append(
            pltpu.make_async_remote_copy(
                src_ref=src, dst_ref=dst, send_sem=halo_send.at[n], recv_sem=halo_recv.at[n],
                device_id=place(*step), device_id_type=MESH,
            )
        )

    def start_halos(late):
        for (step, _, _), copy in zip(messages, halos):
            if step[0]:
                if not late:
                    copy.start()
            else:
                near = lax.rem(gz + step[2] + N_GZ, N_GZ) < 4
                pl.when(jnp.logical_not(near) if late else near)(copy.start)

    start_halos(False)

    def arrived(y, z):
        index = y * N_GZ + z
        pltpu.make_async_copy(send.at[index], got.at[index], recv_sem.at[index]).wait()

    order = ((0, 1), (2, 3), (7, 6), (5, 4))

    def step(n, half):
        for y in order[n]:
            for z in range(4 * half, 4 * half + 4):
                arrived(y, z)
        return spread_step(got, [2 * y + half for y in order[n]], quads, left, table)

    total[...] = step(0, 0)
    for n in range(1, 4):
        total[...] += step(n, 0)

    @pl.when(first)
    def _():
        pl.semaphore_wait(late_sem, 32)

    vertex_copies(range(4, 8), lambda copy: copy.start())
    start_halos(True)

    for copy in halos:
        copy.wait_recv()
    lane = lax.broadcasted_iota(I32, (SY, SZ), 1)
    line = lax.broadcasted_iota(I32, (SY, SZ), 0)
    lane4 = lax.broadcasted_iota(I32, (SX, SZ), 1)
    masks = {
        ("z", 1): lane == 0, ("z", -1): lane == SZ - 1,
        ("z4", 1): lane4 == 0, ("z4", -1): lane4 == SZ - 1,
        ("y", 1): line == 0, ("y", -1): line == SY - 1,
    }
    received = (got_hx, got_hy, got_hz, got_xy, got_xz, got_yz)
    for x in range(SX):
        for i in range(19):
            shifted[i, x] = moved(pop, received, i, x, masks)

    for n in range(3):
        total[...] += step(n, 1)
    for copy in halos:
        copy.wait_send()
    vertex_copies(range(8), lambda copy: copy.wait_send())
    last = total[...] + step(3, 1)
    field = last[0:192, 0:SZ] + (last[192:384, 0:SZ] + last[0:192, SZ : 2 * SZ])
    for c in range(3):
        for x in range(SX):
            spot = (c * SX + x) * SY
            force[c, x] = field[spot : spot + SY]


def collide_kernel(shifted, solid, body, new, force):
    for x in range(SX):
        s = [shifted[i, x] for i in range(19)]
        density = s[0]
        momentum = [None, None, None]
        for i in range(1, 19, 2):
            density = density + (s[i] + s[i + 1])
            gap = s[i] - s[i + 1]
            for axis in range(3):
                c = VEL[i][axis]
                if c:
                    old = momentum[axis]
                    if old is None:
                        momentum[axis] = gap
                    else:
                        momentum[axis] = old + gap if c > 0 else old - gap
        push = [body[c, x] for c in range(3)]
        for c in range(3):
            force[c, x] = push[c]
        inverse = 1.0 / density
        flow = [(momentum[a] + 0.5 * push[a]) * inverse for a in range(3)]
        speed = flow[0] * flow[0] + flow[1] * flow[1] + flow[2] * flow[2]
        work = flow[0] * push[0] + flow[1] * push[1] + flow[2] * push[2]
        wall = solid[x] == 1
        common = density * (1.25 - 1.875 * speed) - 1.125 * work
        square = 5.625 * density
        linear = 3.75 * density
        new[0, x] = jnp.where(wall, s[0], (1.0 / 3.0) * common - 0.25 * s[0])
        for i in range(1, 19, 2):
            weight = 1.0 / 18.0 if i < 7 else 1.0 / 36.0
            a = b = None
            for axis in range(3):
                c = VEL[i][axis]
                if c:
                    if a is None:
                        a, b = flow[axis], push[axis]
                    elif c > 0:
                        a, b = a + flow[axis], b + push[axis]
                    else:
                        a, b = a - flow[axis], b - push[axis]
            even = weight * (common + a * (square * a + 3.375 * b))
            odd = weight * (linear * a + 1.125 * b)
            new[i, x] = jnp.where(wall, s[i + 1], (even + odd) - 0.25 * s[i])
            new[i + 1, x] = jnp.where(wall, s[i], (even - odd) - 0.25 * s[i + 1])


def whole(count):
    return [pl.BlockSpec(memory_space=pltpu.VMEM)] * count


def local(populations, solid_mask, displacement, stiffness, neighbours, owners, stencil_base, stencil_weights):
    def f32(*shape):
        return jax.ShapeDtypeStruct(shape, F32)

    def vmem(*shape):
        return pltpu.VMEM(shape, F32)

    halo = (2, 5, SY, SZ), (2, 5, SX, SZ), (2, 8, 128)
    shifted, body = pl.pallas_call(
        gather_kernel,
        out_shape=(f32(19, SX, SY, SZ), f32(3, SX, SY, SZ)),
        in_specs=[pl.BlockSpec(memory_space=pltpu.HBM)] + whole(6),
        out_specs=tuple(whole(2)),
        scratch_shapes=[
            vmem(19, SX, SY, SZ), vmem(4, 8, 1024), vmem(GROUP, 4, 128), vmem(GROUP, 4, 128),
            *(vmem(*shape) for shape in halo), *(vmem(*shape) for shape in halo),
            vmem(4, SX, SZ), vmem(4, SY, SZ), vmem(4, SX, SZ),
            vmem(16, 4, 4, 128), pltpu.VMEM((384, 256), BF16), pltpu.VMEM((256, 256), BF16), vmem(384, 256),
            pltpu.SemaphoreType.DMA,
            pltpu.SemaphoreType.DMA((GROUP,)),
            pltpu.SemaphoreType.DMA((GROUP,)),
            pltpu.SemaphoreType.DMA((18,)),
            pltpu.SemaphoreType.DMA((18,)),
            pltpu.SemaphoreType.REGULAR,
        ],
        compiler_params=pltpu.CompilerParams(
            collective_id=0, has_side_effects=True, vmem_limit_bytes=16 * 1024 * 1024
        ),
        name="gather",
    )(
        *(pltpu.with_memory_space_constraint(v, pltpu.HBM) for v in (
        populations, displacement, stiffness.reshape(1, 1024), neighbours,
        owners.reshape(1, 1024), stencil_base.reshape(1, 1024), stencil_weights))
    )
    return tuple(
        pl.pallas_call(
            collide_kernel,
            out_shape=(f32(19, SX, SY, SZ), f32(3, SX, SY, SZ)),
            in_specs=whole(3),
            out_specs=tuple(whole(2)),
            compiler_params=pltpu.CompilerParams(vmem_limit_bytes=8 * 1024 * 1024),
            name="collide",
        )(shifted, solid_mask, body)
    )


def solution(mesh):
    placed = (
        P(None, "gx", "gy", "gz"),
        P("gx", "gy", "gz"),
        P(None, ("gx", "gy", "gz")),
        P(("gx", "gy", "gz")),
        P(None, ("gx", "gy", "gz")),
        P(("gx", "gy", "gz"), None),
        P(("gx", "gy", "gz")),
        P(None, ("gx", "gy", "gz")),
    )
    return jax.shard_map(
        local,
        mesh=mesh,
        in_specs=placed,
        out_specs=(P(None, "gx", "gy", "gz"), P(None, "gx", "gy", "gz")),
        check_vma=False,
    )
```

```python
import functools

import jax
import jax.numpy as jnp
import numpy as np
from jax import lax
from jax.experimental import pallas as pl
from jax.experimental.pallas import tpu as pltpu
from jax.sharding import PartitionSpec as P

MESH = pl.DeviceIdType.MESH
F32 = jnp.float32
BF16 = jnp.bfloat16
I32 = jnp.int32

VEL = (
    (0, 0, 0),
    (1, 0, 0), (-1, 0, 0), (0, 1, 0), (0, -1, 0), (0, 0, 1), (0, 0, -1),
    (1, 1, 0), (-1, -1, 0), (1, -1, 0), (-1, 1, 0),
    (1, 0, 1), (-1, 0, -1), (1, 0, -1), (-1, 0, 1),
    (0, 1, 1), (0, -1, -1), (0, 1, -1), (0, -1, 1),
)
SX, SY, SZ = 4, 16, 128
N_GY = N_GZ = 8
GROUP = N_GY * N_GZ
FACE = tuple(
    tuple(tuple(i for i in range(19) if VEL[i][axis] == sign) for sign in (1, -1))
    for axis in range(3)
)
EDGE_XY = (7, 8, 9, 10)
EDGE_XZ = (11, 12, 13, 14)
EDGE_YZ = (15, 16, 17, 18)


def side(sign):
    return 0 if sign > 0 else 1


def face_slot(axis, i):
    s = side(VEL[i][axis])
    return s, FACE[axis][s].index(i)


def bf(x):
    return x.astype(BF16)


def dot_nt(a, b):
    return lax.dot_general(a, b, (((1,), (1,)), ((), ())), preferred_element_type=F32)


def lane_gather(table, index):
    return jnp.take_along_axis(table, index, axis=1, mode="promise_in_bounds")


def pack_faces(pop, hx, hy, hz):
    for s in range(2):
        for k, i in enumerate(FACE[0][s]):
            hx[s, k] = pop[i, 3 if s == 0 else 0]
        row = 15 if s == 0 else 0
        for k, i in enumerate(FACE[1][s]):
            for x in range(SX):
                hy[s, k, x : x + 1, :] = pop[i, x, row : row + 1, :]
        lane = lax.broadcasted_iota(I32, (8, 128), 1)
        edge = 127 if s == 0 else 0
        packed = jnp.zeros((8, 128), F32)
        for k, i in enumerate(FACE[2][s]):
            for x in range(SX):
                for half in range(2):
                    place = 16 * (2 * x + half) + k
                    rolled = pltpu.roll(pop[i, x, 8 * half : 8 * half + 8, :], (place - edge) % 128, 1)
                    packed = jnp.where(lane == place, rolled, packed)
        hz[s] = packed


def pack_vertices(disp, stiff, nbr, owner, base, weights, send, pay):
    lane = lax.broadcasted_iota(I32, (1, 128), 1)
    own = owner[...]
    group_ids = lax.broadcasted_iota(I32, (GROUP, 128), 0)
    member = [jnp.where(own[:, 128 * v : 128 * v + 128] == group_ids, 1.0, 0.0) for v in range(8)]
    before = [jnp.zeros((GROUP, 128), F32)]
    for v in range(7):
        before.append(before[v] + member[v])
    stacked = jnp.concatenate(
        [jnp.concatenate([bf(member[v]), bf(before[v])], axis=1) for v in range(8)], axis=0
    )
    rows = lax.broadcasted_iota(I32, (256, 128), 0)
    cols = lax.broadcasted_iota(I32, (256, 128), 1)
    upto = bf(jnp.where((rows <= cols) | (rows >= 128), 1.0, 0.0))
    running = jnp.dot(stacked, upto, preferred_element_type=F32)
    for v in range(8):
        here = slice(128 * v, 128 * v + 128)
        index = nbr[:, here]
        low, high = index & 127, index >> 7
        for c in range(3):
            total = jnp.zeros((6, 128), F32)
            for k in range(8):
                table = jnp.broadcast_to(disp[c : c + 1, 128 * k : 128 * k + 128], (6, 128))
                total = jnp.where(high == k, lane_gather(table, low), total)
            summed = jnp.sum(total, axis=0, keepdims=True)
            value = stiff[:, here] * (summed - 6.0 * disp[c : c + 1, here])
            pay[c, 0:1, here] = value
            pay[c, 4:5, here] = value
        value = base[:, here].astype(F32)
        pay[3, 0:1, here] = value
        pay[3, 4:5, here] = value
    for l in range(4):
        for i in range(3):
            value = weights[4 * i + l : 4 * i + l + 1, :]
            pay[l, i + 1 : i + 2, :] = value
            pay[l, i + 5 : i + 6, :] = value
    quad_ids = lax.broadcasted_iota(I32, (GROUP // 4, 128), 0)
    slot_ids = lax.broadcasted_iota(I32, (128, 128), 0)
    lefts, rights = [], []
    for v in range(8):
        rank = jnp.sum(member[v] * running[GROUP * v : GROUP * v + GROUP], axis=0, keepdims=True) - 1.0
        own_v = own[:, 128 * v : 128 * v + 128]
        slot = (own_v & 3) * 32 + rank.astype(I32)
        quad = (own_v >> 2) == quad_ids
        lefts.append(
            jnp.concatenate(
                [
                    bf(jnp.where(quad, lane.astype(F32), 0.0)),
                    bf(jnp.where(quad, float(v + 1), 0.0)),
                ],
                axis=0,
            )
        )
        rights.append(bf(jnp.where(slot == slot_ids, 1.0, 0.0)))
    found = dot_nt(jnp.concatenate(lefts, axis=1), jnp.concatenate(rights, axis=1))
    code = (found[0:16] + 128.0 * found[16:32]).astype(I32)
    codes = [code] + [pltpu.roll(code, 32 * j, 1) for j in range(1, 4)]
    lane_quad = lax.broadcasted_iota(I32, (8, 128), 1) >> 5
    for h in range(8):
        picked = []
        for l in range(4):
            pair = jnp.concatenate(
                [jnp.broadcast_to(codes[l][g : g + 1], (4, 128)) for g in (2 * h, 2 * h + 1)], axis=0
            )
            low, high = pair & 127, pair >> 7
            got = jnp.zeros((8, 128), F32)
            for k in range(8):
                got = jnp.where(high == k + 1, lane_gather(pay[l, :, 128 * k : 128 * k + 128], low), got)
            picked.append(got)
        for q in range(4):
            mixed = picked[0]
            for l in range(1, 4):
                mixed = jnp.where(lane_quad == (q + l) % 4, picked[l], mixed)
            if q:
                mixed = pltpu.roll(mixed, 128 - 32 * q, 1)
            send[8 * h + q] = mixed[0:4]
            send[8 * h + 4 + q] = mixed[4:8]


def spread_step(got, sources, quads, left, table):
    lane_quad = lax.broadcasted_iota(I32, (4, 128), 1) >> 5
    iota_y = lax.broadcasted_iota(I32, (SY, 128), 0).astype(F32)
    iota_z = lax.broadcasted_iota(I32, (SZ, 128), 0).astype(F32)
    for n, g in enumerate(sources):
        here = slice(128 * n, 128 * n + 128)
        skewed = [got[4 * g + j] for j in range(4)]
        skewed = [pltpu.roll(skewed[j], 32 * j, 1) if j else skewed[j] for j in range(4)]
        for l in range(4):
            mixed = skewed[0]
            for j in range(1, 4):
                mixed = jnp.where(lane_quad == (l + j) % 4, skewed[j], mixed)
            if l:
                mixed = pltpu.roll(mixed, 128 - 32 * l, 1)
            quads[g, l] = mixed

        def row(p):
            return quads[g, p % 4, p // 4 : p // 4 + 1, :]

        corner = row(3).astype(I32)
        off_y = iota_y - (corner >> 7).astype(F32)
        off_z = iota_z - (corner & 127).astype(F32)
        table_y = jnp.zeros((SY, 128), F32)
        for j in range(4):
            table_y = jnp.where(off_y == float(j), row(8 + j), table_y)
        high = jnp.zeros((SZ, 128), F32)
        low = jnp.zeros((SZ, 128), F32)
        for k in range(4):
            weight = row(12 + k)
            weight_high = bf(weight).astype(F32)
            hit = off_z == float(k)
            high = jnp.where(hit, weight_high, high)
            low = jnp.where(hit, weight - weight_high, low)
        table[0:SZ, here] = bf(high)
        table[SZ : 2 * SZ, here] = bf(low)
        for c in range(3):
            for x in range(SX):
                value = (row(c) * row(4 + x)) * table_y
                value_high = bf(value)
                place = (c * SX + x) * SY
                left[place : place + SY, here] = value_high
                left[192 + place : 192 + place + SY, here] = bf(value - value_high.astype(F32))
    return dot_nt(left[...], table[...])


def moved(pop, halos, i, x, masks):
    hx, hy, hz, exy, exz, eyz = halos
    cx, cy, cz = VEL[i]
    source = x - cx
    inside = 0 <= source < SX
    if inside:
        cells = pop[i, source]
    else:
        cells = hx[face_slot(0, i)]
    if cz:
        cells = pltpu.roll(cells, cz % 128, 1)
        s, k = face_slot(2, i)
        edge = 0 if cz > 0 else 127
        if inside:
            packed = hz[s]
            column = jnp.concatenate(
                [pltpu.roll(packed, (edge - 16 * (2 * source + half) - k) % 128, 1) for half in range(2)],
                axis=0,
            )
        else:
            column = pltpu.roll(exz[EDGE_XZ.index(i)], cz % 128, 1)
        cells = jnp.where(masks["z", cz], column, cells)
    if cy:
        cells = pltpu.roll(cells, cy % 16, 0)
        if inside:
            line = hy[face_slot(1, i)]
            if cz:
                line = pltpu.roll(line, cz % 128, 1)
                beyond = pltpu.roll(eyz[EDGE_YZ.index(i)], cz % 128, 1)
                line = jnp.where(masks["z4", cz], beyond, line)
        else:
            line = exy[EDGE_XY.index(i)]
        line = line[source % SX : source % SX + 1]
        cells = jnp.where(masks["y", cy], jnp.broadcast_to(line, (SY, SZ)), cells)
    return cells


def halo_messages(hx, hy, hz, got_hx, got_hy, got_hz, got_xy, got_xz, got_yz):
    messages = []
    for s, sign in enumerate((1, -1)):
        messages.append(((sign, 0, 0), hx.at[s], got_hx.at[s]))
        messages.append(((0, sign, 0), hy.at[s], got_hy.at[s]))
        messages.append(((0, 0, sign), hz.at[s], got_hz.at[s]))
    for n, i in enumerate(EDGE_XY):
        s, k = face_slot(1, i)
        messages.append((VEL[i], hy.at[s, k], got_xy.at[n]))
    for n, i in enumerate(EDGE_XZ):
        s, k = face_slot(0, i)
        messages.append((VEL[i], hx.at[s, k], got_xz.at[n]))
    for n, i in enumerate(EDGE_YZ):
        s, k = face_slot(1, i)
        messages.append((VEL[i], hy.at[s, k], got_yz.at[n]))
    return messages


def gather_kernel(
    pop_hbm, disp, stiff, nbr, owner, base, weights, shifted, force,
    pop, pay, send, got, hx, hy, hz, got_hx, got_hy, got_hz, got_xy, got_xz, got_yz,
    quads, left, table, total,
    load_sem, send_sem, recv_sem, halo_send, halo_recv, late_sem, go_sem, edge_sem,
):
    gx, gy, gz = lax.axis_index("gx"), lax.axis_index("gy"), lax.axis_index("gz")
    me = gy * N_GZ + gz
    first = gz < 4

    def place(dx, dy, dz):
        return {
            "gx": lax.rem(gx + dx + 8, 8),
            "gy": lax.rem(gy + dy + N_GY, N_GY),
            "gz": lax.rem(gz + dz + N_GZ, N_GZ),
        }

    def signal(semaphore, device):
        pl.semaphore_signal(semaphore, inc=1, device_id=device, device_id_type=MESH)

    messages = halo_messages(hx, hy, hz, got_hx, got_hy, got_hz, got_xy, got_xz, got_yz)
    barrier = pltpu.get_barrier_semaphore()
    outside = [m[0] for m in messages if m[0][0] != 0]

    @pl.when(first)
    def _():
        for t in range(1, GROUP):
            signal(barrier, place(0, t // N_GZ, t % N_GZ))

    def far(step):
        return lax.rem(gz + step[2] + N_GZ, N_GZ) >= 4

    def all_of(*terms):
        return functools.reduce(jnp.logical_and, terms)

    for step in outside:
        if step[2]:
            pl.when(jnp.logical_or(first, far(step)))(functools.partial(signal, barrier, place(*step)))
        else:
            signal(barrier, place(*step))
    load = pltpu.make_async_copy(pop_hbm, pop, load_sem)
    load.start()

    pack_vertices(disp, stiff, nbr, owner, base, weights, send, pay)

    rim = jnp.logical_or(gz == 0, gz == 3)

    @pl.when(rim)
    def _():
        pl.semaphore_wait(barrier, 31 + len(outside) - 2)

    @pl.when(all_of(first, jnp.logical_not(rim)))
    def _():
        pl.semaphore_wait(barrier, 31 + len(outside))

    @pl.when(jnp.logical_not(first))
    def _():
        pl.semaphore_wait(barrier, 32 + len(outside))
        for z in range(4):
            for k in range(8):
                signal(late_sem, {"gx": gx, "gy": lax.rem(gy + k, N_GY), "gz": z})
        for step in outside:
            if step[2]:
                pl.when(jnp.logical_not(far(step)))(functools.partial(signal, edge_sem, place(*step)))

    def vertex_copy(y, z):
        index = y * N_GZ + z
        return pltpu.make_async_remote_copy(
            src_ref=send.at[index], dst_ref=got.at[me],
            send_sem=send_sem.at[index], recv_sem=recv_sem.at[me],
            device_id={"gx": gx, "gy": y, "gz": z}, device_id_type=MESH,
        )

    def vertex_copies(planes, act):
        for z in planes:
            for k in range(8):
                copy = vertex_copy(lax.rem(gy + k, N_GY), z)
                if k:
                    act(copy)
                else:
                    pl.when(gz != z)(functools.partial(act, copy))

    vertex_copies(range(0, 4), lambda copy: copy.start())
    own = pltpu.make_async_copy(send.at[me], got.at[me], recv_sem.at[me])
    own.start()

    load.wait()
    pack_faces(pop, hx, hy, hz)
    halos = []
    for n, (step, src, dst) in enumerate(messages):
        halos.append(
            pltpu.make_async_remote_copy(
                src_ref=src, dst_ref=dst, send_sem=halo_send.at[n], recv_sem=halo_recv.at[n],
                device_id=place(*step), device_id_type=MESH,
            )
        )

    for (step, _, _), copy in zip(messages, halos):
        if step[0] and not step[2]:
            copy.start()
        elif step[0]:
            pl.when(jnp.logical_not(all_of(first, far(step))))(copy.start)
        else:
            pl.when(jnp.logical_not(far(step)))(copy.start)

    def send_to_late():
        vertex_copies(range(4, 8), lambda copy: copy.start())
        for (step, _, _), copy in zip(messages, halos):
            if not step[0]:
                pl.when(far(step))(copy.start)

    @pl.when(jnp.logical_not(first))
    def _():
        pl.semaphore_wait(go_sem, 1)
        send_to_late()

    def arrived(y, z):
        index = y * N_GZ + z
        pltpu.make_async_copy(send.at[index], got.at[index], recv_sem.at[index]).wait()

    order = ((0, 1), (2, 3), (7, 6), (5, 4))

    def step(n, half):
        for y in order[n]:
            for z in range(4 * half, 4 * half + 4):
                arrived(y, z)
        return spread_step(got, [2 * y + half for y in order[n]], quads, left, table)

    total[...] = step(0, 0)
    for n in range(1, 4):
        total[...] += step(n, 0)

    @pl.when(first)
    def _():
        pl.semaphore_wait(late_sem, 32)
        signal(go_sem, {"gx": gx, "gy": gy, "gz": gz + 4})
        send_to_late()

    @pl.when(rim)
    def _():
        pl.semaphore_wait(edge_sem, 2)
        for (step, _, _), copy in zip(messages, halos):
            if step[0] and step[2]:
                pl.when(far(step))(copy.start)

    for copy in halos:
        copy.wait_recv()
    lane = lax.broadcasted_iota(I32, (SY, SZ), 1)
    line = lax.broadcasted_iota(I32, (SY, SZ), 0)
    lane4 = lax.broadcasted_iota(I32, (SX, SZ), 1)
    masks = {
        ("z", 1): lane == 0, ("z", -1): lane == SZ - 1,
        ("z4", 1): lane4 == 0, ("z4", -1): lane4 == SZ - 1,
        ("y", 1): line == 0, ("y", -1): line == SY - 1,
    }
    received = (got_hx, got_hy, got_hz, got_xy, got_xz, got_yz)
    for x in range(SX):
        for i in range(19):
            shifted[i, x] = moved(pop, received, i, x, masks)

    for n in range(3):
        total[...] += step(n, 1)
    for copy in halos:
        copy.wait_send()
    vertex_copies(range(8), lambda copy: copy.wait_send())
    last = total[...] + step(3, 1)
    field = last[0:192, 0:SZ] + (last[192:384, 0:SZ] + last[0:192, SZ : 2 * SZ])
    for c in range(3):
        for x in range(SX):
            spot = (c * SX + x) * SY
            force[c, x] = field[spot : spot + SY]


def collide_kernel(shifted, solid, body, new, force):
    for x in range(SX):
        s = [shifted[i, x] for i in range(19)]
        density = s[0]
        momentum = [None, None, None]
        for i in range(1, 19, 2):
            density = density + (s[i] + s[i + 1])
            gap = s[i] - s[i + 1]
            for axis in range(3):
                c = VEL[i][axis]
                if c:
                    old = momentum[axis]
                    if old is None:
                        momentum[axis] = gap
                    else:
                        momentum[axis] = old + gap if c > 0 else old - gap
        push = [body[c, x] for c in range(3)]
        for c in range(3):
            force[c, x] = push[c]
        inverse = 1.0 / density
        flow = [(momentum[a] + 0.5 * push[a]) * inverse for a in range(3)]
        speed = flow[0] * flow[0] + flow[1] * flow[1] + flow[2] * flow[2]
        work = flow[0] * push[0] + flow[1] * push[1] + flow[2] * push[2]
        wall = solid[x] == 1
        common = density * (1.25 - 1.875 * speed) - 1.125 * work
        square = 5.625 * density
        linear = 3.75 * density
        new[0, x] = jnp.where(wall, s[0], (1.0 / 3.0) * common - 0.25 * s[0])
        for i in range(1, 19, 2):
            weight = 1.0 / 18.0 if i < 7 else 1.0 / 36.0
            a = b = None
            for axis in range(3):
                c = VEL[i][axis]
                if c:
                    if a is None:
                        a, b = flow[axis], push[axis]
                    elif c > 0:
                        a, b = a + flow[axis], b + push[axis]
                    else:
                        a, b = a - flow[axis], b - push[axis]
            even = weight * (common + a * (square * a + 3.375 * b))
            odd = weight * (linear * a + 1.125 * b)
            new[i, x] = jnp.where(wall, s[i + 1], (even + odd) - 0.25 * s[i])
            new[i + 1, x] = jnp.where(wall, s[i], (even - odd) - 0.25 * s[i + 1])


def whole(count):
    return [pl.BlockSpec(memory_space=pltpu.VMEM)] * count


def local(populations, solid_mask, displacement, stiffness, neighbours, owners, stencil_base, stencil_weights):
    def f32(*shape):
        return jax.ShapeDtypeStruct(shape, F32)

    def vmem(*shape):
        return pltpu.VMEM(shape, F32)

    halo = (2, 5, SY, SZ), (2, 5, SX, SZ), (2, 8, 128)
    shifted, body = pl.pallas_call(
        gather_kernel,
        out_shape=(f32(19, SX, SY, SZ), f32(3, SX, SY, SZ)),
        in_specs=[pl.BlockSpec(memory_space=pltpu.HBM)] + whole(6),
        out_specs=tuple(whole(2)),
        scratch_shapes=[
            vmem(19, SX, SY, SZ), vmem(4, 8, 1024), vmem(GROUP, 4, 128), vmem(GROUP, 4, 128),
            *(vmem(*shape) for shape in halo), *(vmem(*shape) for shape in halo),
            vmem(4, SX, SZ), vmem(4, SY, SZ), vmem(4, SX, SZ),
            vmem(16, 4, 4, 128), pltpu.VMEM((384, 256), BF16), pltpu.VMEM((256, 256), BF16), vmem(384, 256),
            pltpu.SemaphoreType.DMA,
            pltpu.SemaphoreType.DMA((GROUP,)),
            pltpu.SemaphoreType.DMA((GROUP,)),
            pltpu.SemaphoreType.DMA((18,)),
            pltpu.SemaphoreType.DMA((18,)),
            pltpu.SemaphoreType.REGULAR,
            pltpu.SemaphoreType.REGULAR,
            pltpu.SemaphoreType.REGULAR,
        ],
        compiler_params=pltpu.CompilerParams(
            collective_id=0, has_side_effects=True, vmem_limit_bytes=16 * 1024 * 1024
        ),
        name="gather",
    )(
        *(pltpu.with_memory_space_constraint(v, pltpu.HBM) for v in (
        populations, displacement, stiffness.reshape(1, 1024), neighbours,
        owners.reshape(1, 1024), stencil_base.reshape(1, 1024), stencil_weights))
    )
    return tuple(
        pl.pallas_call(
            collide_kernel,
            out_shape=(f32(19, SX, SY, SZ), f32(3, SX, SY, SZ)),
            in_specs=whole(3),
            out_specs=tuple(whole(2)),
            compiler_params=pltpu.CompilerParams(vmem_limit_bytes=8 * 1024 * 1024),
            name="collide",
        )(shifted, solid_mask, body)
    )


def solution(mesh):
    placed = (
        P(None, "gx", "gy", "gz"),
        P("gx", "gy", "gz"),
        P(None, ("gx", "gy", "gz")),
        P(("gx", "gy", "gz")),
        P(None, ("gx", "gy", "gz")),
        P(("gx", "gy", "gz"), None),
        P(("gx", "gy", "gz")),
        P(None, ("gx", "gy", "gz")),
    )
    return jax.shard_map(
        local,
        mesh=mesh,
        in_specs=placed,
        out_specs=(P(None, "gx", "gy", "gz"), P(None, "gx", "gy", "gz")),
        check_vma=False,
    )
```

```python
import functools

import jax
import jax.numpy as jnp
import numpy as np
from jax import lax
from jax.experimental import pallas as pl
from jax.experimental.pallas import tpu as pltpu
from jax.sharding import PartitionSpec as P

MESH = pl.DeviceIdType.MESH
F32 = jnp.float32
BF16 = jnp.bfloat16
I32 = jnp.int32

VEL = (
    (0, 0, 0),
    (1, 0, 0), (-1, 0, 0), (0, 1, 0), (0, -1, 0), (0, 0, 1), (0, 0, -1),
    (1, 1, 0), (-1, -1, 0), (1, -1, 0), (-1, 1, 0),
    (1, 0, 1), (-1, 0, -1), (1, 0, -1), (-1, 0, 1),
    (0, 1, 1), (0, -1, -1), (0, 1, -1), (0, -1, 1),
)
SX, SY, SZ = 4, 16, 128
N_GY = N_GZ = 8
EARLY = 2
GROUP = N_GY * N_GZ
FACE = tuple(
    tuple(tuple(i for i in range(19) if VEL[i][axis] == sign) for sign in (1, -1))
    for axis in range(3)
)
EDGE_XY = (7, 8, 9, 10)
EDGE_XZ = (11, 12, 13, 14)
EDGE_YZ = (15, 16, 17, 18)


def side(sign):
    return 0 if sign > 0 else 1


def face_slot(axis, i):
    s = side(VEL[i][axis])
    return s, FACE[axis][s].index(i)


def bf(x):
    return x.astype(BF16)


def dot_nt(a, b):
    return lax.dot_general(a, b, (((1,), (1,)), ((), ())), preferred_element_type=F32)


def lane_gather(table, index):
    return jnp.take_along_axis(table, index, axis=1, mode="promise_in_bounds")


def pack_faces(pop, hx, hy, hz):
    for s in range(2):
        for k, i in enumerate(FACE[0][s]):
            hx[s, k] = pop[i, 3 if s == 0 else 0]
        row = 15 if s == 0 else 0
        for k, i in enumerate(FACE[1][s]):
            for x in range(SX):
                hy[s, k, x : x + 1, :] = pop[i, x, row : row + 1, :]
        lane = lax.broadcasted_iota(I32, (8, 128), 1)
        edge = 127 if s == 0 else 0
        packed = jnp.zeros((8, 128), F32)
        for k, i in enumerate(FACE[2][s]):
            for x in range(SX):
                for half in range(2):
                    place = 16 * (2 * x + half) + k
                    rolled = pltpu.roll(pop[i, x, 8 * half : 8 * half + 8, :], (place - edge) % 128, 1)
                    packed = jnp.where(lane == place, rolled, packed)
        hz[s] = packed


def pack_vertices(disp, stiff, nbr, owner, base, weights, send, pay):
    lane = lax.broadcasted_iota(I32, (1, 128), 1)
    own = owner[...]
    group_ids = lax.broadcasted_iota(I32, (GROUP, 128), 0)
    member = [jnp.where(own[:, 128 * v : 128 * v + 128] == group_ids, 1.0, 0.0) for v in range(8)]
    before = [jnp.zeros((GROUP, 128), F32)]
    for v in range(7):
        before.append(before[v] + member[v])
    stacked = jnp.concatenate(
        [jnp.concatenate([bf(member[v]), bf(before[v])], axis=1) for v in range(8)], axis=0
    )
    rows = lax.broadcasted_iota(I32, (256, 128), 0)
    cols = lax.broadcasted_iota(I32, (256, 128), 1)
    upto = bf(jnp.where((rows <= cols) | (rows >= 128), 1.0, 0.0))
    running = jnp.dot(stacked, upto, preferred_element_type=F32)
    for v in range(8):
        here = slice(128 * v, 128 * v + 128)
        index = nbr[:, here]
        low, high = index & 127, index >> 7
        for c in range(3):
            total = jnp.zeros((6, 128), F32)
            for k in range(8):
                table = jnp.broadcast_to(disp[c : c + 1, 128 * k : 128 * k + 128], (6, 128))
                total = jnp.where(high == k, lane_gather(table, low), total)
            summed = jnp.sum(total, axis=0, keepdims=True)
            value = stiff[:, here] * (summed - 6.0 * disp[c : c + 1, here])
            pay[c, 0:1, here] = value
            pay[c, 4:5, here] = value
        value = base[:, here].astype(F32)
        pay[3, 0:1, here] = value
        pay[3, 4:5, here] = value
    for l in range(4):
        for i in range(3):
            value = weights[4 * i + l : 4 * i + l + 1, :]
            pay[l, i + 1 : i + 2, :] = value
            pay[l, i + 5 : i + 6, :] = value
    quad_ids = lax.broadcasted_iota(I32, (GROUP // 4, 128), 0)
    slot_ids = lax.broadcasted_iota(I32, (128, 128), 0)
    lefts, rights = [], []
    for v in range(8):
        rank = jnp.sum(member[v] * running[GROUP * v : GROUP * v + GROUP], axis=0, keepdims=True) - 1.0
        own_v = own[:, 128 * v : 128 * v + 128]
        slot = (own_v & 3) * 32 + rank.astype(I32)
        quad = (own_v >> 2) == quad_ids
        lefts.append(
            jnp.concatenate(
                [
                    bf(jnp.where(quad, lane.astype(F32), 0.0)),
                    bf(jnp.where(quad, float(v + 1), 0.0)),
                ],
                axis=0,
            )
        )
        rights.append(bf(jnp.where(slot == slot_ids, 1.0, 0.0)))
    found = dot_nt(jnp.concatenate(lefts, axis=1), jnp.concatenate(rights, axis=1))
    code = (found[0:16] + 128.0 * found[16:32]).astype(I32)
    codes = [code] + [pltpu.roll(code, 32 * j, 1) for j in range(1, 4)]
    lane_quad = lax.broadcasted_iota(I32, (8, 128), 1) >> 5
    for h in range(8):
        picked = []
        for l in range(4):
            pair = jnp.concatenate(
                [jnp.broadcast_to(codes[l][g : g + 1], (4, 128)) for g in (2 * h, 2 * h + 1)], axis=0
            )
            low, high = pair & 127, pair >> 7
            got = jnp.zeros((8, 128), F32)
            for k in range(8):
                got = jnp.where(high == k + 1, lane_gather(pay[l, :, 128 * k : 128 * k + 128], low), got)
            picked.append(got)
        for q in range(4):
            mixed = picked[0]
            for l in range(1, 4):
                mixed = jnp.where(lane_quad == (q + l) % 4, picked[l], mixed)
            if q:
                mixed = pltpu.roll(mixed, 128 - 32 * q, 1)
            send[8 * h + q] = mixed[0:4]
            send[8 * h + 4 + q] = mixed[4:8]


def spread_step(got, sources, quads, left, table):
    lane_quad = lax.broadcasted_iota(I32, (4, 128), 1) >> 5
    iota_y = lax.broadcasted_iota(I32, (SY, 128), 0).astype(F32)
    iota_z = lax.broadcasted_iota(I32, (SZ, 128), 0).astype(F32)
    for n, g in enumerate(sources):
        here = slice(128 * n, 128 * n + 128)
        skewed = [got[4 * g + j] for j in range(4)]
        skewed = [pltpu.roll(skewed[j], 32 * j, 1) if j else skewed[j] for j in range(4)]
        for l in range(4):
            mixed = skewed[0]
            for j in range(1, 4):
                mixed = jnp.where(lane_quad == (l + j) % 4, skewed[j], mixed)
            if l:
                mixed = pltpu.roll(mixed, 128 - 32 * l, 1)
            quads[g, l] = mixed

        def row(p):
            return quads[g, p % 4, p // 4 : p // 4 + 1, :]

        corner = row(3).astype(I32)
        off_y = iota_y - (corner >> 7).astype(F32)
        off_z = iota_z - (corner & 127).astype(F32)
        table_y = jnp.zeros((SY, 128), F32)
        for j in range(4):
            table_y = jnp.where(off_y == float(j), row(8 + j), table_y)
        high = jnp.zeros((SZ, 128), F32)
        low = jnp.zeros((SZ, 128), F32)
        for k in range(4):
            weight = row(12 + k)
            weight_high = bf(weight).astype(F32)
            hit = off_z == float(k)
            high = jnp.where(hit, weight_high, high)
            low = jnp.where(hit, weight - weight_high, low)
        table[0:SZ, here] = bf(high)
        table[SZ : 2 * SZ, here] = bf(low)
        for c in range(3):
            for x in range(SX):
                value = (row(c) * row(4 + x)) * table_y
                value_high = bf(value)
                place = (c * SX + x) * SY
                left[place : place + SY, here] = value_high
                left[192 + place : 192 + place + SY, here] = bf(value - value_high.astype(F32))
    return dot_nt(left[...], table[...])


def moved(pop, halos, i, x, masks):
    hx, hy, hz, exy, exz, eyz = halos
    cx, cy, cz = VEL[i]
    source = x - cx
    inside = 0 <= source < SX
    if inside:
        cells = pop[i, source]
    else:
        cells = hx[face_slot(0, i)]
    if cz:
        cells = pltpu.roll(cells, cz % 128, 1)
        s, k = face_slot(2, i)
        edge = 0 if cz > 0 else 127
        if inside:
            packed = hz[s]
            column = jnp.concatenate(
                [pltpu.roll(packed, (edge - 16 * (2 * source + half) - k) % 128, 1) for half in range(2)],
                axis=0,
            )
        else:
            column = pltpu.roll(exz[EDGE_XZ.index(i)], cz % 128, 1)
        cells = jnp.where(masks["z", cz], column, cells)
    if cy:
        cells = pltpu.roll(cells, cy % 16, 0)
        if inside:
            line = hy[face_slot(1, i)]
            if cz:
                line = pltpu.roll(line, cz % 128, 1)
                beyond = pltpu.roll(eyz[EDGE_YZ.index(i)], cz % 128, 1)
                line = jnp.where(masks["z4", cz], beyond, line)
        else:
            line = exy[EDGE_XY.index(i)]
        row = source if inside else (7 if cy > 0 else 0)
        line = line[row : row + 1]
        cells = jnp.where(masks["y", cy], jnp.broadcast_to(line, (SY, SZ)), cells)
    return cells


def halo_messages(hx, hy, hz, got_hx, got_hy, got_hz, got_xy, got_xz, got_yz):
    messages = []
    for s, sign in enumerate((1, -1)):
        messages.append(((sign, 0, 0), hx.at[s], got_hx.at[s]))
        messages.append(((0, sign, 0), hy.at[s], got_hy.at[s]))
        messages.append(((0, 0, sign), hz.at[s], got_hz.at[s]))
    for n, i in enumerate(EDGE_XY):
        half = 8 if VEL[i][1] > 0 else 0
        messages.append(((0, VEL[i][1], 0), got_hx.at[face_slot(0, i)].at[pl.ds(half, 8)], got_xy.at[n]))
    for n, i in enumerate(EDGE_XZ):
        messages.append(((0, 0, VEL[i][2]), got_hx.at[face_slot(0, i)], got_xz.at[n]))
    for n, i in enumerate(EDGE_YZ):
        s, k = face_slot(1, i)
        messages.append((VEL[i], hy.at[s, k], got_yz.at[n]))
    return messages


def gather_kernel(
    pop_in, disp_in, stiff_in, nbr_in, owner_in, base_in, weights_in,
    shifted, force, pop, disp, stiff, nbr, owner, base, weights, pay, send, got, hx, hy, hz, got_hx, got_hy, got_hz, got_xy, got_xz, got_yz,
    quads, left, table, total,
    load_sem, send_sem, recv_sem, halo_send, halo_recv, late_sem, go_sem,
):
    gx, gy, gz = lax.axis_index("gx"), lax.axis_index("gy"), lax.axis_index("gz")
    me = gy * N_GZ + gz
    first = gz < EARLY

    def place(dx, dy, dz):
        return {
            "gx": lax.rem(gx + dx + 8, 8),
            "gy": lax.rem(gy + dy + N_GY, N_GY),
            "gz": lax.rem(gz + dz + N_GZ, N_GZ),
        }

    def signal(semaphore, device):
        pl.semaphore_signal(semaphore, inc=1, device_id=device, device_id_type=MESH)

    messages = halo_messages(hx, hy, hz, got_hx, got_hy, got_hz, got_xy, got_xz, got_yz)
    barrier = pltpu.get_barrier_semaphore()
    outside = [m[0] for m in messages if m[0][0] != 0]

    @pl.when(first)
    def _():
        for t in range(1, GROUP):
            signal(barrier, place(0, t // N_GZ, t % N_GZ))

    def far(step):
        return lax.rem(gz + step[2] + N_GZ, N_GZ) >= EARLY

    for step in outside:
        signal(barrier, place(*step))
    pairs = (
        (disp_in, disp), (nbr_in, nbr), (owner_in, owner), (stiff_in, stiff), (base_in, base),
        (weights_in, weights), (pop_in, pop),
    )
    loads = [pltpu.make_async_copy(src, dst, load_sem.at[n]) for n, (src, dst) in enumerate(pairs)]
    for copy in loads:
        copy.start()
    for copy in loads[:-1]:
        copy.wait()
    pack_vertices(disp, stiff, nbr, owner, base, weights, send, pay)

    @pl.when(first)
    def _():
        pl.semaphore_wait(barrier, N_GY * EARLY - 1 + len(outside))

    @pl.when(jnp.logical_not(first))
    def _():
        pl.semaphore_wait(barrier, N_GY * EARLY + len(outside))
        for z in range(EARLY):
            for k in range(8):
                signal(late_sem.at[me], {"gx": gx, "gy": lax.rem(gy + k, N_GY), "gz": z})

    def vertex_copy(y, z):
        index = y * N_GZ + z
        return pltpu.make_async_remote_copy(
            src_ref=send.at[index], dst_ref=got.at[me],
            send_sem=send_sem.at[index], recv_sem=recv_sem.at[me],
            device_id={"gx": gx, "gy": y, "gz": z}, device_id_type=MESH,
        )

    def vertex_copies(planes, act):
        for z in planes:
            for k in (4, 3, 5, 2, 6, 1, 7, 0):
                copy = vertex_copy(lax.rem(gy + k, N_GY), z)
                if k:
                    act(copy)
                else:
                    pl.when(gz != z)(functools.partial(act, copy))

    vertex_copies(range(EARLY), lambda copy: copy.start())
    own = pltpu.make_async_copy(send.at[me], got.at[me], recv_sem.at[me])
    own.start()

    loads[-1].wait()
    pack_faces(pop, hx, hy, hz)
    halos = []
    for n, (step, src, dst) in enumerate(messages):
        halos.append(
            pltpu.make_async_remote_copy(
                src_ref=src, dst_ref=dst, send_sem=halo_send.at[n], recv_sem=halo_recv.at[n],
                device_id=place(*step), device_id_type=MESH,
            )
        )

    passed_on = [6 <= n < 14 for n in range(len(messages))]

    def near_halos(again):
        for n, ((step, _, _), copy) in enumerate(zip(messages, halos)):
            if not step[0] and passed_on[n] == again:
                pl.when(jnp.logical_not(far(step)))(copy.start)

    for copy in halos[0], halos[3]:
        copy.start()
    near_halos(False)
    for copy in halos[0], halos[3]:
        copy.wait_recv()
    near_halos(True)

    def halos_to(z):
        for dz in (-1, 0, 1):

            @pl.when(lax.rem(gz + dz + N_GZ, N_GZ) == z)
            def _():
                for (step, _, _), copy in zip(messages, halos):
                    if step[0] == 0 and step[2] == dz:
                        copy.start()

    def serve(z, rows):
        for k in rows:
            y = lax.rem(gy + k, N_GY)
            pl.semaphore_wait(late_sem.at[y * N_GZ + z], 1)
            vertex_copy(y, z).start()

    def pass_on(z):
        for j in range(3):
            signal(go_sem.at[z], {"gx": gx, "gy": gy, "gz": 7 - j + gz * (2 * j - 5)})

    def own_row(planes, brick):
        @pl.when(gz == brick)
        def _():
            for z in planes:
                serve(z, (0,))

    near_rows, far_rows = (1, 7, 2, 6), (3, 5, 4)

    @pl.when(first)
    def _():
        own_row(range(2, 5), 1)
        own_row(range(5, 8), 0)
        for z in range(EARLY, 4):
            own_row([z], 0)
            serve(z, near_rows + far_rows)
            pass_on(z)
            halos_to(z)
        for z in range(4, 8):
            own_row([z], 0 if z == 4 else 1)
            serve(z, near_rows)
            halos_to(z)

    @pl.when(jnp.logical_not(first))
    def _():
        for z in range(EARLY, 8):
            pl.semaphore_wait(go_sem.at[z], 1)
            vertex_copies([z], lambda copy: copy.start())
            halos_to(z)

    def arrived(y, z):
        index = y * N_GZ + z
        pltpu.make_async_copy(send.at[index], got.at[index], recv_sem.at[index]).wait()

    order = ((0, 1), (2, 3), (7, 6), (5, 4))

    def step(n, half):
        for y in order[n]:
            for z in range(4 * half, 4 * half + 4):
                arrived(y, z)
        return spread_step(got, [2 * y + half for y in order[n]], quads, left, table)

    total[...] = step(0, 0)

    @pl.when(first)
    def _():
        for z in range(4, 8):
            serve(z, far_rows)
            pass_on(z)

    for n in range(1, 4):
        total[...] += step(n, 0)
    for n, copy in enumerate(halos):
        if n not in (0, 3):
            copy.wait_recv()
    lane = lax.broadcasted_iota(I32, (SY, SZ), 1)
    line = lax.broadcasted_iota(I32, (SY, SZ), 0)
    lane4 = lax.broadcasted_iota(I32, (SX, SZ), 1)
    masks = {
        ("z", 1): lane == 0, ("z", -1): lane == SZ - 1,
        ("z4", 1): lane4 == 0, ("z4", -1): lane4 == SZ - 1,
        ("y", 1): line == 0, ("y", -1): line == SY - 1,
    }
    received = (got_hx, got_hy, got_hz, got_xy, got_xz, got_yz)
    for x in range(SX):
        for i in range(19):
            shifted[i, x] = moved(pop, received, i, x, masks)

    for n in range(3):
        total[...] += step(n, 1)
    for copy in halos:
        copy.wait_send()
    vertex_copies(range(8), lambda copy: copy.wait_send())
    last = total[...] + step(3, 1)
    field = last[0:192, 0:SZ] + (last[192:384, 0:SZ] + last[0:192, SZ : 2 * SZ])
    for c in range(3):
        for x in range(SX):
            spot = (c * SX + x) * SY
            force[c, x] = field[spot : spot + SY]


def collide_kernel(shifted, solid, body, new_out, force_out, new, sems):
    copies = [pltpu.make_async_copy(body, force_out, sems.at[SX])]
    copies[0].start()
    for x in range(SX):
        s = [shifted[i, x] for i in range(19)]
        density = s[0]
        momentum = [None, None, None]
        for i in range(1, 19, 2):
            density = density + (s[i] + s[i + 1])
            gap = s[i] - s[i + 1]
            for axis in range(3):
                c = VEL[i][axis]
                if c:
                    old = momentum[axis]
                    if old is None:
                        momentum[axis] = gap
                    else:
                        momentum[axis] = old + gap if c > 0 else old - gap
        push = [body[c, x] for c in range(3)]
        inverse = 1.0 / density
        flow = [(momentum[a] + 0.5 * push[a]) * inverse for a in range(3)]
        speed = flow[0] * flow[0] + flow[1] * flow[1] + flow[2] * flow[2]
        work = flow[0] * push[0] + flow[1] * push[1] + flow[2] * push[2]
        wall = solid[x] == 1
        common = density * (1.25 - 1.875 * speed) - 1.125 * work
        square = 5.625 * density
        linear = 3.75 * density
        new[0, x] = jnp.where(wall, s[0], (1.0 / 3.0) * common - 0.25 * s[0])
        for i in range(1, 19, 2):
            weight = 1.0 / 18.0 if i < 7 else 1.0 / 36.0
            a = b = None
            for axis in range(3):
                c = VEL[i][axis]
                if c:
                    if a is None:
                        a, b = flow[axis], push[axis]
                    elif c > 0:
                        a, b = a + flow[axis], b + push[axis]
                    else:
                        a, b = a - flow[axis], b - push[axis]
            even = weight * (common + a * (square * a + 3.375 * b))
            odd = weight * (linear * a + 1.125 * b)
            new[i, x] = jnp.where(wall, s[i + 1], (even + odd) - 0.25 * s[i])
            new[i + 1, x] = jnp.where(wall, s[i], (even - odd) - 0.25 * s[i + 1])
        copies.append(pltpu.make_async_copy(new.at[:, x], new_out.at[:, x], sems.at[x]))
        copies[-1].start()
    for copy in copies:
        copy.wait()


def whole(count):
    return [pl.BlockSpec(memory_space=pltpu.VMEM)] * count


def local(populations, solid_mask, displacement, stiffness, neighbours, owners, stencil_base, stencil_weights):
    def f32(*shape):
        return jax.ShapeDtypeStruct(shape, F32)

    def vmem(*shape):
        return pltpu.VMEM(shape, F32)

    halo = (2, 5, SY, SZ), (2, 5, SX, SZ), (2, 8, 128)
    shifted, body = pl.pallas_call(
        gather_kernel,
        out_shape=(f32(19, SX, SY, SZ), f32(3, SX, SY, SZ)),
        in_specs=[pl.BlockSpec(memory_space=pltpu.HBM)] * 7,
        out_specs=tuple(whole(2)),
        scratch_shapes=[
            vmem(19, SX, SY, SZ), vmem(3, 1024), vmem(1, 1024), pltpu.VMEM((6, 1024), I32), pltpu.VMEM((1, 1024), I32),
            pltpu.VMEM((1, 1024), I32), vmem(12, 1024), vmem(4, 8, 1024), vmem(GROUP, 4, 128), vmem(GROUP, 4, 128),
            *(vmem(*shape) for shape in halo), *(vmem(*shape) for shape in halo),
            vmem(4, 8, SZ), vmem(4, SY, SZ), vmem(4, SX, SZ),
            vmem(16, 4, 4, 128), pltpu.VMEM((384, 256), BF16), pltpu.VMEM((256, 256), BF16), vmem(384, 256),
            pltpu.SemaphoreType.DMA((7,)),
            pltpu.SemaphoreType.DMA((GROUP,)),
            pltpu.SemaphoreType.DMA((GROUP,)),
            pltpu.SemaphoreType.DMA((18,)),
            pltpu.SemaphoreType.DMA((18,)),
            pltpu.SemaphoreType.REGULAR((GROUP,)),
            pltpu.SemaphoreType.REGULAR((N_GZ,)),
        ],
        compiler_params=pltpu.CompilerParams(
            collective_id=0, has_side_effects=True, vmem_limit_bytes=16 * 1024 * 1024
        ),
        name="gather",
    )(
        *(pltpu.with_memory_space_constraint(v, pltpu.HBM) for v in (
        populations, displacement, stiffness.reshape(1, 1024), neighbours,
        owners.reshape(1, 1024), stencil_base.reshape(1, 1024), stencil_weights))
    )
    return tuple(
        pl.pallas_call(
            collide_kernel,
            out_shape=(f32(19, SX, SY, SZ), f32(3, SX, SY, SZ)),
            in_specs=whole(3),
            out_specs=(pl.BlockSpec(memory_space=pltpu.HBM),) * 2,
            scratch_shapes=[vmem(19, SX, SY, SZ), pltpu.SemaphoreType.DMA((SX + 1,))],
            compiler_params=pltpu.CompilerParams(vmem_limit_bytes=8 * 1024 * 1024),
            name="collide",
        )(shifted, solid_mask, body)
    )


def solution(mesh):
    placed = (
        P(None, "gx", "gy", "gz"),
        P("gx", "gy", "gz"),
        P(None, ("gx", "gy", "gz")),
        P(("gx", "gy", "gz")),
        P(None, ("gx", "gy", "gz")),
        P(("gx", "gy", "gz"), None),
        P(("gx", "gy", "gz")),
        P(None, ("gx", "gy", "gz")),
    )
    return jax.shard_map(
        local,
        mesh=mesh,
        in_specs=placed,
        out_specs=(P(None, "gx", "gy", "gz"), P(None, "gx", "gy", "gz")),
        check_vma=False,
    )
```

```python
import functools

import jax
import jax.numpy as jnp
import numpy as np
from jax import lax
from jax.experimental import pallas as pl
from jax.experimental.pallas import tpu as pltpu
from jax.sharding import PartitionSpec as P

MESH = pl.DeviceIdType.MESH
F32 = jnp.float32
BF16 = jnp.bfloat16
I32 = jnp.int32

VEL = (
    (0, 0, 0),
    (1, 0, 0), (-1, 0, 0), (0, 1, 0), (0, -1, 0), (0, 0, 1), (0, 0, -1),
    (1, 1, 0), (-1, -1, 0), (1, -1, 0), (-1, 1, 0),
    (1, 0, 1), (-1, 0, -1), (1, 0, -1), (-1, 0, 1),
    (0, 1, 1), (0, -1, -1), (0, 1, -1), (0, -1, 1),
)
SX, SY, SZ = 4, 16, 128
N_GY = N_GZ = 8
EARLY = 3
GROUP = N_GY * N_GZ
FACE = tuple(
    tuple(tuple(i for i in range(19) if VEL[i][axis] == sign) for sign in (1, -1))
    for axis in range(3)
)
EDGE_XY = (7, 8, 9, 10)
EDGE_XZ = (11, 12, 13, 14)
EDGE_YZ = (15, 16, 17, 18)


def side(sign):
    return 0 if sign > 0 else 1


def face_slot(axis, i):
    s = side(VEL[i][axis])
    return s, FACE[axis][s].index(i)


def bf(x):
    return x.astype(BF16)


def dot_nt(a, b):
    return lax.dot_general(a, b, (((1,), (1,)), ((), ())), preferred_element_type=F32)


def lane_gather(table, index):
    return jnp.take_along_axis(table, index, axis=1, mode="promise_in_bounds")


def pack_faces(pop, hx, hy, hz):
    for s in range(2):
        for k, i in enumerate(FACE[0][s]):
            hx[s, k] = pop[i, 3 if s == 0 else 0]
        row = 15 if s == 0 else 0
        for k, i in enumerate(FACE[1][s]):
            for x in range(SX):
                hy[s, k, x : x + 1, :] = pop[i, x, row : row + 1, :]
        lane = lax.broadcasted_iota(I32, (8, 128), 1)
        edge = 127 if s == 0 else 0
        packed = jnp.zeros((8, 128), F32)
        for k, i in enumerate(FACE[2][s]):
            for x in range(SX):
                for half in range(2):
                    place = 16 * (2 * x + half) + k
                    rolled = pltpu.roll(pop[i, x, 8 * half : 8 * half + 8, :], (place - edge) % 128, 1)
                    packed = jnp.where(lane == place, rolled, packed)
        hz[s] = packed


def pack_vertices(disp, stiff, nbr, owner, base, weights, send, pay):
    lane = lax.broadcasted_iota(I32, (1, 128), 1)
    own = owner[...]
    group_ids = lax.broadcasted_iota(I32, (GROUP, 128), 0)
    member = [jnp.where(own[:, 128 * v : 128 * v + 128] == group_ids, 1.0, 0.0) for v in range(8)]
    before = [jnp.zeros((GROUP, 128), F32)]
    for v in range(7):
        before.append(before[v] + member[v])
    stacked = jnp.concatenate(
        [jnp.concatenate([bf(member[v]), bf(before[v])], axis=1) for v in range(8)], axis=0
    )
    rows = lax.broadcasted_iota(I32, (256, 128), 0)
    cols = lax.broadcasted_iota(I32, (256, 128), 1)
    upto = bf(jnp.where((rows <= cols) | (rows >= 128), 1.0, 0.0))
    running = jnp.dot(stacked, upto, preferred_element_type=F32)
    for v in range(8):
        here = slice(128 * v, 128 * v + 128)
        index = nbr[:, here]
        low, high = index & 127, index >> 7
        for c in range(3):
            total = jnp.zeros((6, 128), F32)
            for k in range(8):
                table = jnp.broadcast_to(disp[c : c + 1, 128 * k : 128 * k + 128], (6, 128))
                total = jnp.where(high == k, lane_gather(table, low), total)
            summed = jnp.sum(total, axis=0, keepdims=True)
            value = stiff[:, here] * (summed - 6.0 * disp[c : c + 1, here])
            pay[c, 0:1, here] = value
            pay[c, 4:5, here] = value
        value = base[:, here].astype(F32)
        pay[3, 0:1, here] = value
        pay[3, 4:5, here] = value
    for l in range(4):
        for i in range(3):
            value = weights[4 * i + l : 4 * i + l + 1, :]
            pay[l, i + 1 : i + 2, :] = value
            pay[l, i + 5 : i + 6, :] = value
    quad_ids = lax.broadcasted_iota(I32, (GROUP // 4, 128), 0)
    slot_ids = lax.broadcasted_iota(I32, (128, 128), 0)
    lefts, rights = [], []
    for v in range(8):
        rank = jnp.sum(member[v] * running[GROUP * v : GROUP * v + GROUP], axis=0, keepdims=True) - 1.0
        own_v = own[:, 128 * v : 128 * v + 128]
        slot = (own_v & 3) * 32 + rank.astype(I32)
        quad = (own_v >> 2) == quad_ids
        lefts.append(
            jnp.concatenate(
                [
                    bf(jnp.where(quad, lane.astype(F32), 0.0)),
                    bf(jnp.where(quad, float(v + 1), 0.0)),
                ],
                axis=0,
            )
        )
        rights.append(bf(jnp.where(slot == slot_ids, 1.0, 0.0)))
    found = dot_nt(jnp.concatenate(lefts, axis=1), jnp.concatenate(rights, axis=1))
    code = (found[0:16] + 128.0 * found[16:32]).astype(I32)
    codes = [code] + [pltpu.roll(code, 32 * j, 1) for j in range(1, 4)]
    lane_quad = lax.broadcasted_iota(I32, (8, 128), 1) >> 5
    for h in range(8):
        picked = []
        for l in range(4):
            pair = jnp.concatenate(
                [jnp.broadcast_to(codes[l][g : g + 1], (4, 128)) for g in (2 * h, 2 * h + 1)], axis=0
            )
            low, high = pair & 127, pair >> 7
            got = jnp.zeros((8, 128), F32)
            for k in range(8):
                got = jnp.where(high == k + 1, lane_gather(pay[l, :, 128 * k : 128 * k + 128], low), got)
            picked.append(got)
        for q in range(4):
            mixed = picked[0]
            for l in range(1, 4):
                mixed = jnp.where(lane_quad == (q + l) % 4, picked[l], mixed)
            if q:
                mixed = pltpu.roll(mixed, 128 - 32 * q, 1)
            send[8 * h + q] = mixed[0:4]
            send[8 * h + 4 + q] = mixed[4:8]


def spread_step(got, sources, quads, left, table):
    lane_quad = lax.broadcasted_iota(I32, (4, 128), 1) >> 5
    iota_y = lax.broadcasted_iota(I32, (SY, 128), 0).astype(F32)
    iota_z = lax.broadcasted_iota(I32, (SZ, 128), 0).astype(F32)
    for n, g in enumerate(sources):
        here = slice(128 * n, 128 * n + 128)
        skewed = [got[4 * g + j] for j in range(4)]
        skewed = [pltpu.roll(skewed[j], 32 * j, 1) if j else skewed[j] for j in range(4)]
        for l in range(4):
            mixed = skewed[0]
            for j in range(1, 4):
                mixed = jnp.where(lane_quad == (l + j) % 4, skewed[j], mixed)
            if l:
                mixed = pltpu.roll(mixed, 128 - 32 * l, 1)
            quads[g, l] = mixed

        def row(p):
            return quads[g, p % 4, p // 4 : p // 4 + 1, :]

        corner = row(3).astype(I32)
        off_y = iota_y - (corner >> 7).astype(F32)
        off_z = iota_z - (corner & 127).astype(F32)
        table_y = jnp.zeros((SY, 128), F32)
        for j in range(4):
            table_y = jnp.where(off_y == float(j), row(8 + j), table_y)
        high = jnp.zeros((SZ, 128), F32)
        low = jnp.zeros((SZ, 128), F32)
        for k in range(4):
            weight = row(12 + k)
            weight_high = bf(weight).astype(F32)
            hit = off_z == float(k)
            high = jnp.where(hit, weight_high, high)
            low = jnp.where(hit, weight - weight_high, low)
        table[0:SZ, here] = bf(high)
        table[SZ : 2 * SZ, here] = bf(low)
        for c in range(3):
            for x in range(SX):
                value = (row(c) * row(4 + x)) * table_y
                value_high = bf(value)
                place = (c * SX + x) * SY
                left[place : place + SY, here] = value_high
                left[192 + place : 192 + place + SY, here] = bf(value - value_high.astype(F32))
    return dot_nt(left[...], table[...])


def moved(pop, halos, i, x, masks):
    hx, hy, hz, exy, exz, eyz = halos
    cx, cy, cz = VEL[i]
    source = x - cx
    inside = 0 <= source < SX
    if inside:
        cells = pop[i, source]
    else:
        cells = hx[face_slot(0, i)]
    if cz:
        cells = pltpu.roll(cells, cz % 128, 1)
        s, k = face_slot(2, i)
        edge = 0 if cz > 0 else 127
        if inside:
            packed = hz[s]
            column = jnp.concatenate(
                [pltpu.roll(packed, (edge - 16 * (2 * source + half) - k) % 128, 1) for half in range(2)],
                axis=0,
            )
        else:
            column = pltpu.roll(exz[EDGE_XZ.index(i)], cz % 128, 1)
        cells = jnp.where(masks["z", cz], column, cells)
    if cy:
        cells = pltpu.roll(cells, cy % 16, 0)
        if inside:
            line = hy[face_slot(1, i)]
            if cz:
                line = pltpu.roll(line, cz % 128, 1)
                beyond = pltpu.roll(eyz[EDGE_YZ.index(i)], cz % 128, 1)
                line = jnp.where(masks["z4", cz], beyond, line)
        else:
            line = exy[EDGE_XY.index(i)]
        row = source if inside else (7 if cy > 0 else 0)
        line = line[row : row + 1]
        cells = jnp.where(masks["y", cy], jnp.broadcast_to(line, (SY, SZ)), cells)
    return cells


def halo_messages(hx, hy, hz, got_hx, got_hy, got_hz, got_xy, got_xz, got_yz):
    messages = []
    for s, sign in enumerate((1, -1)):
        messages.append(((sign, 0, 0), hx.at[s], got_hx.at[s]))
        messages.append(((0, sign, 0), hy.at[s], got_hy.at[s]))
        messages.append(((0, 0, sign), hz.at[s], got_hz.at[s]))
    for n, i in enumerate(EDGE_XY):
        half = 8 if VEL[i][1] > 0 else 0
        messages.append(((0, VEL[i][1], 0), got_hx.at[face_slot(0, i)].at[pl.ds(half, 8)], got_xy.at[n]))
    for n, i in enumerate(EDGE_XZ):
        messages.append(((0, 0, VEL[i][2]), got_hx.at[face_slot(0, i)], got_xz.at[n]))
    for n, i in enumerate(EDGE_YZ):
        s, k = face_slot(1, i)
        messages.append((VEL[i], hy.at[s, k], got_yz.at[n]))
    return messages


def gather_kernel(
    pop_in, disp_in, stiff_in, nbr_in, owner_in, base_in, weights_in,
    shifted, force, pop, disp, stiff, nbr, owner, base, weights, pay, send, got, hx, hy, hz, got_hx, got_hy, got_hz, got_xy, got_xz, got_yz,
    quads, left, table, total,
    load_sem, send_sem, recv_sem, halo_send, halo_recv, late_sem, go_sem,
):
    gx, gy, gz = lax.axis_index("gx"), lax.axis_index("gy"), lax.axis_index("gz")
    me = gy * N_GZ + gz
    first = gz < EARLY

    def place(dx, dy, dz):
        return {
            "gx": lax.rem(gx + dx + 8, 8),
            "gy": lax.rem(gy + dy + N_GY, N_GY),
            "gz": lax.rem(gz + dz + N_GZ, N_GZ),
        }

    def signal(semaphore, device):
        pl.semaphore_signal(semaphore, inc=1, device_id=device, device_id_type=MESH)

    messages = halo_messages(hx, hy, hz, got_hx, got_hy, got_hz, got_xy, got_xz, got_yz)
    barrier = pltpu.get_barrier_semaphore()
    outside = [m[0] for m in messages if m[0][0] != 0]

    @pl.when(first)
    def _():
        for t in range(1, GROUP):
            signal(barrier, place(0, t // N_GZ, t % N_GZ))

    def far(step):
        return lax.rem(gz + step[2] + N_GZ, N_GZ) >= EARLY

    for step in outside:
        signal(barrier, place(*step))
    pairs = (
        (disp_in, disp), (nbr_in, nbr), (owner_in, owner), (stiff_in, stiff), (base_in, base),
        (weights_in, weights), (pop_in, pop),
    )
    loads = [pltpu.make_async_copy(src, dst, load_sem.at[n]) for n, (src, dst) in enumerate(pairs)]
    for copy in loads:
        copy.start()
    for copy in loads[:-1]:
        copy.wait()
    def announce():
        pl.semaphore_wait(barrier, N_GY * EARLY + len(outside))
        for z in range(EARLY):
            for k in (4, 3, 5, 2, 6, 1, 7, 0):
                signal(late_sem.at[me], {"gx": gx, "gy": lax.rem(gy + k, N_GY), "gz": z})

    slow = jnp.logical_or(gx == 0, gy < 2)
    pl.when(jnp.logical_not(jnp.logical_or(first, slow)))(announce)
    pack_vertices(disp, stiff, nbr, owner, base, weights, send, pay)
    pl.when(jnp.logical_and(jnp.logical_not(first), slow))(announce)

    @pl.when(first)
    def _():
        pl.semaphore_wait(barrier, N_GY * EARLY - 1 + len(outside))

    def vertex_copy(y, z):
        index = y * N_GZ + z
        return pltpu.make_async_remote_copy(
            src_ref=send.at[index], dst_ref=got.at[me],
            send_sem=send_sem.at[index], recv_sem=recv_sem.at[me],
            device_id={"gx": gx, "gy": y, "gz": z}, device_id_type=MESH,
        )

    def vertex_copies(planes, act):
        for z in planes:
            for k in (4, 3, 5, 2, 6, 1, 7, 0):
                copy = vertex_copy(lax.rem(gy + k, N_GY), z)
                if k:
                    act(copy)
                else:
                    pl.when(gz != z)(functools.partial(act, copy))

    vertex_copies([0], lambda copy: copy.start())
    own = pltpu.make_async_copy(send.at[me], got.at[me], recv_sem.at[me])
    own.start()

    loads[-1].wait()
    pack_faces(pop, hx, hy, hz)
    halos = []
    for n, (step, src, dst) in enumerate(messages):
        halos.append(
            pltpu.make_async_remote_copy(
                src_ref=src, dst_ref=dst, send_sem=halo_send.at[n], recv_sem=halo_recv.at[n],
                device_id=place(*step), device_id_type=MESH,
            )
        )

    passed_on = [6 <= n < 14 for n in range(len(messages))]

    def near_halos(again):
        for n, ((step, _, _), copy) in enumerate(zip(messages, halos)):
            if not step[0] and passed_on[n] == again:
                pl.when(jnp.logical_not(far(step)))(copy.start)

    for copy in halos[0], halos[3]:
        copy.start()
    vertex_copies(range(1, EARLY), lambda copy: copy.start())
    near_halos(False)
    for copy in halos[0], halos[3]:
        copy.wait_recv()
    near_halos(True)

    def halos_to(z):
        for dz in (-1, 0, 1):

            @pl.when(lax.rem(gz + dz + N_GZ, N_GZ) == z)
            def _():
                for (step, _, _), copy in zip(messages, halos):
                    if step[0] == 0 and step[2] == dz:
                        copy.start()

    def serve(z, rows):
        for k in rows:
            y = lax.rem(gy + k, N_GY)
            pl.semaphore_wait(late_sem.at[y * N_GZ + z], 1)
            vertex_copy(y, z).start()

    words = ((EARLY - 1, (3, 4)), (0, (7, 6, 5)))

    def pass_on(z):
        for brick, planes in words:

            @pl.when(gz == brick)
            def _():
                for to in planes:
                    signal(go_sem.at[z], {"gx": gx, "gy": gy, "gz": to})

    def rest_of_own_row(z):
        for brick, planes in words:
            if z in planes:
                pl.when(gz != brick)(lambda: serve(z, (0,)))

    near_rows, far_rows = (1, 7, 2, 6), (3, 5, 4)

    @pl.when(first)
    def _():
        for brick, planes in words:

            @pl.when(gz == brick)
            def _():
                for z in planes:
                    serve(z, (0,))

        for z in range(EARLY, 4):
            rest_of_own_row(z)
            serve(z, near_rows + far_rows)
            pass_on(z)
            halos_to(z)
        for z in range(4, 8):
            rest_of_own_row(z)
            serve(z, near_rows)
            halos_to(z)

    @pl.when(jnp.logical_not(first))
    def _():
        for z in range(EARLY, 8):
            pl.semaphore_wait(go_sem.at[z], 1)
            vertex_copies([z], lambda copy: copy.start())
            halos_to(z)

    def arrived(y, z):
        index = y * N_GZ + z
        pltpu.make_async_copy(send.at[index], got.at[index], recv_sem.at[index]).wait()

    order = ((0, 1), (2, 3), (7, 6), (5, 4))

    def step(n, half):
        for y in order[n]:
            for z in range(4 * half, 4 * half + 4):
                arrived(y, z)
        return spread_step(got, [2 * y + half for y in order[n]], quads, left, table)

    total[...] = step(0, 0)

    @pl.when(first)
    def _():
        for z in range(4, 8):
            serve(z, far_rows)
            pass_on(z)

    for n in range(1, 4):
        total[...] += step(n, 0)
    for n, copy in enumerate(halos):
        if n not in (0, 3):
            copy.wait_recv()
    lane = lax.broadcasted_iota(I32, (SY, SZ), 1)
    line = lax.broadcasted_iota(I32, (SY, SZ), 0)
    lane4 = lax.broadcasted_iota(I32, (SX, SZ), 1)
    masks = {
        ("z", 1): lane == 0, ("z", -1): lane == SZ - 1,
        ("z4", 1): lane4 == 0, ("z4", -1): lane4 == SZ - 1,
        ("y", 1): line == 0, ("y", -1): line == SY - 1,
    }
    received = (got_hx, got_hy, got_hz, got_xy, got_xz, got_yz)
    for x in range(SX):
        for i in range(19):
            shifted[i, x] = moved(pop, received, i, x, masks)

    for n in range(3):
        total[...] += step(n, 1)
    for copy in halos:
        copy.wait_send()
    vertex_copies(range(8), lambda copy: copy.wait_send())
    last = total[...] + step(3, 1)
    field = last[0:192, 0:SZ] + (last[192:384, 0:SZ] + last[0:192, SZ : 2 * SZ])
    for c in range(3):
        for x in range(SX):
            spot = (c * SX + x) * SY
            force[c, x] = field[spot : spot + SY]


def collide_kernel(shifted, solid, body, new_out, force_out, new, sems):
    copies = [pltpu.make_async_copy(body, force_out, sems.at[SX])]
    copies[0].start()
    for x in range(SX):
        s = [shifted[i, x] for i in range(19)]
        density = s[0]
        momentum = [None, None, None]
        for i in range(1, 19, 2):
            density = density + (s[i] + s[i + 1])
            gap = s[i] - s[i + 1]
            for axis in range(3):
                c = VEL[i][axis]
                if c:
                    old = momentum[axis]
                    if old is None:
                        momentum[axis] = gap
                    else:
                        momentum[axis] = old + gap if c > 0 else old - gap
        push = [body[c, x] for c in range(3)]
        inverse = 1.0 / density
        flow = [(momentum[a] + 0.5 * push[a]) * inverse for a in range(3)]
        speed = flow[0] * flow[0] + flow[1] * flow[1] + flow[2] * flow[2]
        work = flow[0] * push[0] + flow[1] * push[1] + flow[2] * push[2]
        wall = solid[x] == 1
        common = density * (1.25 - 1.875 * speed) - 1.125 * work
        square = 5.625 * density
        linear = 3.75 * density
        new[0, x] = jnp.where(wall, s[0], (1.0 / 3.0) * common - 0.25 * s[0])
        for i in range(1, 19, 2):
            weight = 1.0 / 18.0 if i < 7 else 1.0 / 36.0
            a = b = None
            for axis in range(3):
                c = VEL[i][axis]
                if c:
                    if a is None:
                        a, b = flow[axis], push[axis]
                    elif c > 0:
                        a, b = a + flow[axis], b + push[axis]
                    else:
                        a, b = a - flow[axis], b - push[axis]
            even = weight * (common + a * (square * a + 3.375 * b))
            odd = weight * (linear * a + 1.125 * b)
            new[i, x] = jnp.where(wall, s[i + 1], (even + odd) - 0.25 * s[i])
            new[i + 1, x] = jnp.where(wall, s[i], (even - odd) - 0.25 * s[i + 1])
        copies.append(pltpu.make_async_copy(new.at[:, x], new_out.at[:, x], sems.at[x]))
        copies[-1].start()
    for copy in copies:
        copy.wait()


def whole(count):
    return [pl.BlockSpec(memory_space=pltpu.VMEM)] * count


def local(populations, solid_mask, displacement, stiffness, neighbours, owners, stencil_base, stencil_weights):
    def f32(*shape):
        return jax.ShapeDtypeStruct(shape, F32)

    def vmem(*shape):
        return pltpu.VMEM(shape, F32)

    halo = (2, 5, SY, SZ), (2, 5, SX, SZ), (2, 8, 128)
    shifted, body = pl.pallas_call(
        gather_kernel,
        out_shape=(f32(19, SX, SY, SZ), f32(3, SX, SY, SZ)),
        in_specs=[pl.BlockSpec(memory_space=pltpu.HBM)] * 7,
        out_specs=tuple(whole(2)),
        scratch_shapes=[
            vmem(19, SX, SY, SZ), vmem(3, 1024), vmem(1, 1024), pltpu.VMEM((6, 1024), I32), pltpu.VMEM((1, 1024), I32),
            pltpu.VMEM((1, 1024), I32), vmem(12, 1024), vmem(4, 8, 1024), vmem(GROUP, 4, 128), vmem(GROUP, 4, 128),
            *(vmem(*shape) for shape in halo), *(vmem(*shape) for shape in halo),
            vmem(4, 8, SZ), vmem(4, SY, SZ), vmem(4, SX, SZ),
            vmem(16, 4, 4, 128), pltpu.VMEM((384, 256), BF16), pltpu.VMEM((256, 256), BF16), vmem(384, 256),
            pltpu.SemaphoreType.DMA((7,)),
            pltpu.SemaphoreType.DMA((GROUP,)),
            pltpu.SemaphoreType.DMA((GROUP,)),
            pltpu.SemaphoreType.DMA((18,)),
            pltpu.SemaphoreType.DMA((18,)),
            pltpu.SemaphoreType.REGULAR((GROUP,)),
            pltpu.SemaphoreType.REGULAR((N_GZ,)),
        ],
        compiler_params=pltpu.CompilerParams(
            collective_id=0, has_side_effects=True, vmem_limit_bytes=16 * 1024 * 1024
        ),
        name="gather",
    )(
        *(pltpu.with_memory_space_constraint(v, pltpu.HBM) for v in (
        populations, displacement, stiffness.reshape(1, 1024), neighbours,
        owners.reshape(1, 1024), stencil_base.reshape(1, 1024), stencil_weights))
    )
    return tuple(
        pl.pallas_call(
            collide_kernel,
            out_shape=(f32(19, SX, SY, SZ), f32(3, SX, SY, SZ)),
            in_specs=whole(3),
            out_specs=(pl.BlockSpec(memory_space=pltpu.HBM),) * 2,
            scratch_shapes=[vmem(19, SX, SY, SZ), pltpu.SemaphoreType.DMA((SX + 1,))],
            compiler_params=pltpu.CompilerParams(vmem_limit_bytes=8 * 1024 * 1024),
            name="collide",
        )(shifted, solid_mask, body)
    )


def solution(mesh):
    placed = (
        P(None, "gx", "gy", "gz"),
        P("gx", "gy", "gz"),
        P(None, ("gx", "gy", "gz")),
        P(("gx", "gy", "gz")),
        P(None, ("gx", "gy", "gz")),
        P(("gx", "gy", "gz"), None),
        P(("gx", "gy", "gz")),
        P(None, ("gx", "gy", "gz")),
    )
    return jax.shard_map(
        local,
        mesh=mesh,
        in_specs=placed,
        out_specs=(P(None, "gx", "gy", "gz"), P(None, "gx", "gy", "gz")),
        check_vma=False,
    )
```

```python
import functools

import jax
import jax.numpy as jnp
import numpy as np
from jax import lax
from jax.experimental import pallas as pl
from jax.experimental.pallas import tpu as pltpu
from jax.sharding import PartitionSpec as P

MESH = pl.DeviceIdType.MESH
F32 = jnp.float32
BF16 = jnp.bfloat16
I32 = jnp.int32

VEL = (
    (0, 0, 0),
    (1, 0, 0), (-1, 0, 0), (0, 1, 0), (0, -1, 0), (0, 0, 1), (0, 0, -1),
    (1, 1, 0), (-1, -1, 0), (1, -1, 0), (-1, 1, 0),
    (1, 0, 1), (-1, 0, -1), (1, 0, -1), (-1, 0, 1),
    (0, 1, 1), (0, -1, -1), (0, 1, -1), (0, -1, 1),
)
SX, SY, SZ = 4, 16, 128
N_GY = N_GZ = 8
EARLY = 3
GROUP = N_GY * N_GZ
FACE = tuple(
    tuple(tuple(i for i in range(19) if VEL[i][axis] == sign) for sign in (1, -1))
    for axis in range(3)
)
EDGE_XY = (7, 8, 9, 10)
EDGE_XZ = (11, 12, 13, 14)
EDGE_YZ = (15, 16, 17, 18)


def side(sign):
    return 0 if sign > 0 else 1


def face_slot(axis, i):
    s = side(VEL[i][axis])
    return s, FACE[axis][s].index(i)


def bf(x):
    return x.astype(BF16)


def dot_nt(a, b):
    return lax.dot_general(a, b, (((1,), (1,)), ((), ())), preferred_element_type=F32)


def lane_gather(table, index):
    return jnp.take_along_axis(table, index, axis=1, mode="promise_in_bounds")


def pack_faces(pop, hx, hy, hz):
    for s in range(2):
        for k, i in enumerate(FACE[0][s]):
            hx[s, k] = pop[i, 3 if s == 0 else 0]
        row = 15 if s == 0 else 0
        for k, i in enumerate(FACE[1][s]):
            for x in range(SX):
                hy[s, k, x : x + 1, :] = pop[i, x, row : row + 1, :]
        lane = lax.broadcasted_iota(I32, (8, 128), 1)
        edge = 127 if s == 0 else 0
        packed = jnp.zeros((8, 128), F32)
        for k, i in enumerate(FACE[2][s]):
            for x in range(SX):
                for half in range(2):
                    place = 16 * (2 * x + half) + k
                    rolled = pltpu.roll(pop[i, x, 8 * half : 8 * half + 8, :], (place - edge) % 128, 1)
                    packed = jnp.where(lane == place, rolled, packed)
        hz[s] = packed


def pack_vertices(disp, stiff, nbr, owner, base, weights, send, pay):
    lane = lax.broadcasted_iota(I32, (1, 128), 1)
    own = owner[...]
    group_ids = lax.broadcasted_iota(I32, (GROUP, 128), 0)
    member = [jnp.where(own[:, 128 * v : 128 * v + 128] == group_ids, 1.0, 0.0) for v in range(8)]
    before = [jnp.zeros((GROUP, 128), F32)]
    for v in range(7):
        before.append(before[v] + member[v])
    stacked = jnp.concatenate(
        [jnp.concatenate([bf(member[v]), bf(before[v])], axis=1) for v in range(8)], axis=0
    )
    rows = lax.broadcasted_iota(I32, (256, 128), 0)
    cols = lax.broadcasted_iota(I32, (256, 128), 1)
    upto = bf(jnp.where((rows <= cols) | (rows >= 128), 1.0, 0.0))
    running = jnp.dot(stacked, upto, preferred_element_type=F32)
    for v in range(8):
        here = slice(128 * v, 128 * v + 128)
        index = nbr[:, here]
        low, high = index & 127, index >> 7
        for c in range(3):
            total = jnp.zeros((6, 128), F32)
            for k in range(8):
                table = jnp.broadcast_to(disp[c : c + 1, 128 * k : 128 * k + 128], (6, 128))
                total = jnp.where(high == k, lane_gather(table, low), total)
            summed = jnp.sum(total, axis=0, keepdims=True)
            value = stiff[:, here] * (summed - 6.0 * disp[c : c + 1, here])
            pay[c, 0:1, here] = value
            pay[c, 4:5, here] = value
        value = base[:, here].astype(F32)
        pay[3, 0:1, here] = value
        pay[3, 4:5, here] = value
    for l in range(4):
        for i in range(3):
            value = weights[4 * i + l : 4 * i + l + 1, :]
            pay[l, i + 1 : i + 2, :] = value
            pay[l, i + 5 : i + 6, :] = value
    quad_ids = lax.broadcasted_iota(I32, (GROUP // 4, 128), 0)
    slot_ids = lax.broadcasted_iota(I32, (128, 128), 0)
    lefts, rights = [], []
    for v in range(8):
        rank = jnp.sum(member[v] * running[GROUP * v : GROUP * v + GROUP], axis=0, keepdims=True) - 1.0
        own_v = own[:, 128 * v : 128 * v + 128]
        slot = (own_v & 3) * 32 + rank.astype(I32)
        quad = (own_v >> 2) == quad_ids
        lefts.append(
            jnp.concatenate(
                [
                    bf(jnp.where(quad, lane.astype(F32), 0.0)),
                    bf(jnp.where(quad, float(v + 1), 0.0)),
                ],
                axis=0,
            )
        )
        rights.append(bf(jnp.where(slot == slot_ids, 1.0, 0.0)))
    found = dot_nt(jnp.concatenate(lefts, axis=1), jnp.concatenate(rights, axis=1))
    code = (found[0:16] + 128.0 * found[16:32]).astype(I32)
    codes = [code] + [pltpu.roll(code, 32 * j, 1) for j in range(1, 4)]
    lane_quad = lax.broadcasted_iota(I32, (8, 128), 1) >> 5
    for h in range(8):
        picked = []
        for l in range(4):
            pair = jnp.concatenate(
                [jnp.broadcast_to(codes[l][g : g + 1], (4, 128)) for g in (2 * h, 2 * h + 1)], axis=0
            )
            low, high = pair & 127, pair >> 7
            got = jnp.zeros((8, 128), F32)
            for k in range(8):
                got = jnp.where(high == k + 1, lane_gather(pay[l, :, 128 * k : 128 * k + 128], low), got)
            picked.append(got)
        for q in range(4):
            mixed = picked[0]
            for l in range(1, 4):
                mixed = jnp.where(lane_quad == (q + l) % 4, picked[l], mixed)
            if q:
                mixed = pltpu.roll(mixed, 128 - 32 * q, 1)
            send[8 * h + q] = mixed[0:4]
            send[8 * h + 4 + q] = mixed[4:8]


def spread_step(got, sources, quads, left, table):
    lane_quad = lax.broadcasted_iota(I32, (4, 128), 1) >> 5
    iota_y = lax.broadcasted_iota(I32, (SY, 128), 0).astype(F32)
    iota_z = lax.broadcasted_iota(I32, (SZ, 128), 0).astype(F32)
    for n, g in enumerate(sources):
        here = slice(128 * n, 128 * n + 128)
        skewed = [got[4 * g + j] for j in range(4)]
        skewed = [pltpu.roll(skewed[j], 32 * j, 1) if j else skewed[j] for j in range(4)]
        for l in range(4):
            mixed = skewed[0]
            for j in range(1, 4):
                mixed = jnp.where(lane_quad == (l + j) % 4, skewed[j], mixed)
            if l:
                mixed = pltpu.roll(mixed, 128 - 32 * l, 1)
            quads[g, l] = mixed

        def row(p):
            return quads[g, p % 4, p // 4 : p // 4 + 1, :]

        corner = row(3).astype(I32)
        off_y = iota_y - (corner >> 7).astype(F32)
        off_z = iota_z - (corner & 127).astype(F32)
        table_y = jnp.zeros((SY, 128), F32)
        for j in range(4):
            table_y = jnp.where(off_y == float(j), row(8 + j), table_y)
        high = jnp.zeros((SZ, 128), F32)
        low = jnp.zeros((SZ, 128), F32)
        for k in range(4):
            weight = row(12 + k)
            weight_high = bf(weight).astype(F32)
            hit = off_z == float(k)
            high = jnp.where(hit, weight_high, high)
            low = jnp.where(hit, weight - weight_high, low)
        table[0:SZ, here] = bf(high)
        table[SZ : 2 * SZ, here] = bf(low)
        for c in range(3):
            for x in range(SX):
                value = (row(c) * row(4 + x)) * table_y
                value_high = bf(value)
                place = (c * SX + x) * SY
                left[place : place + SY, here] = value_high
                left[192 + place : 192 + place + SY, here] = bf(value - value_high.astype(F32))
    return dot_nt(left[...], table[...])


def moved(pop, halos, i, x, masks):
    hx, hy, hz, exy, exz, eyz = halos
    cx, cy, cz = VEL[i]
    source = x - cx
    inside = 0 <= source < SX
    if inside:
        cells = pop[i, source]
    else:
        cells = hx[face_slot(0, i)]
    if cz:
        cells = pltpu.roll(cells, cz % 128, 1)
        s, k = face_slot(2, i)
        edge = 0 if cz > 0 else 127
        if inside:
            packed = hz[s]
            column = jnp.concatenate(
                [pltpu.roll(packed, (edge - 16 * (2 * source + half) - k) % 128, 1) for half in range(2)],
                axis=0,
            )
        else:
            column = pltpu.roll(exz[EDGE_XZ.index(i)], cz % 128, 1)
        cells = jnp.where(masks["z", cz], column, cells)
    if cy:
        cells = pltpu.roll(cells, cy % 16, 0)
        if inside:
            line = hy[face_slot(1, i)]
            if cz:
                line = pltpu.roll(line, cz % 128, 1)
                beyond = pltpu.roll(eyz[EDGE_YZ.index(i)], cz % 128, 1)
                line = jnp.where(masks["z4", cz], beyond, line)
        else:
            line = exy[EDGE_XY.index(i)]
        row = source if inside else (7 if cy > 0 else 0)
        line = line[row : row + 1]
        cells = jnp.where(masks["y", cy], jnp.broadcast_to(line, (SY, SZ)), cells)
    return cells


def halo_messages(hx, hy, hz, got_hx, got_hy, got_hz, got_xy, got_xz, got_yz):
    messages = []
    for s, sign in enumerate((1, -1)):
        messages.append(((sign, 0, 0), hx.at[s], got_hx.at[s]))
        messages.append(((0, sign, 0), hy.at[s], got_hy.at[s]))
        messages.append(((0, 0, sign), hz.at[s], got_hz.at[s]))
    for n, i in enumerate(EDGE_XY):
        half = 8 if VEL[i][1] > 0 else 0
        messages.append(((0, VEL[i][1], 0), got_hx.at[face_slot(0, i)].at[pl.ds(half, 8)], got_xy.at[n]))
    for n, i in enumerate(EDGE_XZ):
        messages.append(((0, 0, VEL[i][2]), got_hx.at[face_slot(0, i)], got_xz.at[n]))
    for n, i in enumerate(EDGE_YZ):
        s, k = face_slot(1, i)
        messages.append((VEL[i], hy.at[s, k], got_yz.at[n]))
    return messages


def gather_kernel(
    pop_in, disp_in, stiff_in, nbr_in, owner_in, base_in, weights_in,
    shifted, force, pop, disp, stiff, nbr, owner, base, weights, pay, send, got, hx, hy, hz, got_hx, got_hy, got_hz, got_xy, got_xz, got_yz,
    quads, left, table, total,
    load_sem, send_sem, recv_sem, halo_send, halo_recv, late_sem, go_sem,
):
    gx, gy, gz = lax.axis_index("gx"), lax.axis_index("gy"), lax.axis_index("gz")
    me = gy * N_GZ + gz
    first = gz < EARLY

    def place(dx, dy, dz):
        return {
            "gx": lax.rem(gx + dx + 8, 8),
            "gy": lax.rem(gy + dy + N_GY, N_GY),
            "gz": lax.rem(gz + dz + N_GZ, N_GZ),
        }

    def signal(semaphore, device):
        pl.semaphore_signal(semaphore, inc=1, device_id=device, device_id_type=MESH)

    messages = halo_messages(hx, hy, hz, got_hx, got_hy, got_hz, got_xy, got_xz, got_yz)
    barrier = pltpu.get_barrier_semaphore()
    outside = [m[0] for m in messages if m[0][0] != 0]

    @pl.when(first)
    def _():
        for t in range(1, GROUP):
            signal(barrier, place(0, t // N_GZ, t % N_GZ))

    def far(step):
        return lax.rem(gz + step[2] + N_GZ, N_GZ) >= EARLY

    for step in outside:
        signal(barrier, place(*step))
    pairs = (
        (disp_in, disp), (nbr_in, nbr), (owner_in, owner), (stiff_in, stiff), (base_in, base),
        (weights_in, weights), (pop_in, pop),
    )
    loads = [pltpu.make_async_copy(src, dst, load_sem.at[n]) for n, (src, dst) in enumerate(pairs)]
    for copy in loads:
        copy.start()
    for copy in loads[:-1]:
        copy.wait()
    def announce():
        pl.semaphore_wait(barrier, N_GY * EARLY + len(outside))
        for z in range(EARLY):
            for k in (4, 3, 5, 2, 6, 1, 7, 0):
                signal(late_sem.at[me], {"gx": gx, "gy": lax.rem(gy + k, N_GY), "gz": z})

    slow = jnp.logical_or(gx == 0, jnp.logical_or(gy < 2, gy == 7))
    pl.when(jnp.logical_not(jnp.logical_or(first, slow)))(announce)
    pack_vertices(disp, stiff, nbr, owner, base, weights, send, pay)
    pl.when(jnp.logical_and(jnp.logical_not(first), slow))(announce)

    @pl.when(first)
    def _():
        pl.semaphore_wait(barrier, N_GY * EARLY - 1 + len(outside))

    def vertex_copy(y, z):
        index = y * N_GZ + z
        return pltpu.make_async_remote_copy(
            src_ref=send.at[index], dst_ref=got.at[me],
            send_sem=send_sem.at[index], recv_sem=recv_sem.at[me],
            device_id={"gx": gx, "gy": y, "gz": z}, device_id_type=MESH,
        )

    def vertex_copies(planes, act):
        for z in planes:
            for k in (4, 3, 5, 2, 6, 1, 7, 0):
                copy = vertex_copy(lax.rem(gy + k, N_GY), z)
                if k:
                    act(copy)
                else:
                    pl.when(gz != z)(functools.partial(act, copy))

    vertex_copies([0], lambda copy: copy.start())
    own = pltpu.make_async_copy(send.at[me], got.at[me], recv_sem.at[me])
    own.start()

    loads[-1].wait()
    pack_faces(pop, hx, hy, hz)
    halos = []
    for n, (step, src, dst) in enumerate(messages):
        halos.append(
            pltpu.make_async_remote_copy(
                src_ref=src, dst_ref=dst, send_sem=halo_send.at[n], recv_sem=halo_recv.at[n],
                device_id=place(*step), device_id_type=MESH,
            )
        )

    passed_on = [6 <= n < 14 for n in range(len(messages))]

    def near_halos(again):
        for n, ((step, _, _), copy) in enumerate(zip(messages, halos)):
            if not step[0] and passed_on[n] == again:
                pl.when(jnp.logical_not(far(step)))(copy.start)

    for copy in halos[0], halos[3]:
        copy.start()
    near_halos(False)
    vertex_copies(range(1, EARLY), lambda copy: copy.start())
    for copy in halos[0], halos[3]:
        copy.wait_recv()
    near_halos(True)

    def halos_to(z):
        for dz in (-1, 0, 1):

            @pl.when(lax.rem(gz + dz + N_GZ, N_GZ) == z)
            def _():
                for (step, _, _), copy in zip(messages, halos):
                    if step[0] == 0 and step[2] == dz:
                        copy.start()

    def serve(z, rows):
        for k in rows:
            y = lax.rem(gy + k, N_GY)
            pl.semaphore_wait(late_sem.at[y * N_GZ + z], 1)
            vertex_copy(y, z).start()

    words = ((EARLY - 1, (3, 4)), (0, (7, 6, 5)))

    def pass_on(z):
        for brick, planes in words:

            @pl.when(gz == brick)
            def _():
                for to in planes:
                    signal(go_sem.at[z], {"gx": gx, "gy": gy, "gz": to})

    def rest_of_own_row(z):
        for brick, planes in words:
            if z in planes:
                pl.when(gz != brick)(lambda: serve(z, (0,)))

    near_rows, far_rows = (1, 7, 2, 6), (3, 5, 4)

    @pl.when(first)
    def _():
        for brick, planes in words:

            @pl.when(gz == brick)
            def _():
                for z in planes:
                    serve(z, (0,))

        for z in range(EARLY, 4):
            rest_of_own_row(z)
            serve(z, near_rows + far_rows)
            pass_on(z)
            halos_to(z)
        for z in range(4, 8):
            rest_of_own_row(z)
            serve(z, near_rows)
            halos_to(z)

    @pl.when(jnp.logical_not(first))
    def _():
        for z in range(EARLY, 8):
            pl.semaphore_wait(go_sem.at[z], 1)
            vertex_copies([z], lambda copy: copy.start())
            halos_to(z)

    def arrived(y, z):
        index = y * N_GZ + z
        pltpu.make_async_copy(send.at[index], got.at[index], recv_sem.at[index]).wait()

    order = ((0, 1), (2, 3), (7, 6), (5, 4))

    def step(n, half):
        for y in order[n]:
            for z in range(4 * half, 4 * half + 4):
                arrived(y, z)
        return spread_step(got, [2 * y + half for y in order[n]], quads, left, table)

    total[...] = step(0, 0)

    @pl.when(first)
    def _():
        for z in range(4, 8):
            serve(z, far_rows)
            pass_on(z)

    for n in range(1, 4):
        total[...] += step(n, 0)
    for n, copy in enumerate(halos):
        if n not in (0, 3):
            copy.wait_recv()
    lane = lax.broadcasted_iota(I32, (SY, SZ), 1)
    line = lax.broadcasted_iota(I32, (SY, SZ), 0)
    lane4 = lax.broadcasted_iota(I32, (SX, SZ), 1)
    masks = {
        ("z", 1): lane == 0, ("z", -1): lane == SZ - 1,
        ("z4", 1): lane4 == 0, ("z4", -1): lane4 == SZ - 1,
        ("y", 1): line == 0, ("y", -1): line == SY - 1,
    }
    received = (got_hx, got_hy, got_hz, got_xy, got_xz, got_yz)
    for x in range(SX):
        for i in range(19):
            shifted[i, x] = moved(pop, received, i, x, masks)

    for n in range(3):
        total[...] += step(n, 1)
    for copy in halos:
        copy.wait_send()
    vertex_copies(range(8), lambda copy: copy.wait_send())
    last = total[...] + step(3, 1)
    field = last[0:192, 0:SZ] + (last[192:384, 0:SZ] + last[0:192, SZ : 2 * SZ])
    for c in range(3):
        for x in range(SX):
            spot = (c * SX + x) * SY
            force[c, x] = field[spot : spot + SY]


def collide_kernel(shifted, solid, body, new_out, force_out, new, sems):
    copies = [pltpu.make_async_copy(body, force_out, sems.at[SX])]
    copies[0].start()
    for x in range(SX):
        s = [shifted[i, x] for i in range(19)]
        density = s[0]
        momentum = [None, None, None]
        for i in range(1, 19, 2):
            density = density + (s[i] + s[i + 1])
            gap = s[i] - s[i + 1]
            for axis in range(3):
                c = VEL[i][axis]
                if c:
                    old = momentum[axis]
                    if old is None:
                        momentum[axis] = gap
                    else:
                        momentum[axis] = old + gap if c > 0 else old - gap
        push = [body[c, x] for c in range(3)]
        inverse = 1.0 / density
        flow = [(momentum[a] + 0.5 * push[a]) * inverse for a in range(3)]
        speed = flow[0] * flow[0] + flow[1] * flow[1] + flow[2] * flow[2]
        work = flow[0] * push[0] + flow[1] * push[1] + flow[2] * push[2]
        wall = solid[x] == 1
        common = density * (1.25 - 1.875 * speed) - 1.125 * work
        square = 5.625 * density
        linear = 3.75 * density
        new[0, x] = jnp.where(wall, s[0], (1.0 / 3.0) * common - 0.25 * s[0])
        for i in range(1, 19, 2):
            weight = 1.0 / 18.0 if i < 7 else 1.0 / 36.0
            a = b = None
            for axis in range(3):
                c = VEL[i][axis]
                if c:
                    if a is None:
                        a, b = flow[axis], push[axis]
                    elif c > 0:
                        a, b = a + flow[axis], b + push[axis]
                    else:
                        a, b = a - flow[axis], b - push[axis]
            even = weight * (common + a * (square * a + 3.375 * b))
            odd = weight * (linear * a + 1.125 * b)
            new[i, x] = jnp.where(wall, s[i + 1], (even + odd) - 0.25 * s[i])
            new[i + 1, x] = jnp.where(wall, s[i], (even - odd) - 0.25 * s[i + 1])
        copies.append(pltpu.make_async_copy(new.at[:, x], new_out.at[:, x], sems.at[x]))
        copies[-1].start()
    for copy in copies:
        copy.wait()


def whole(count):
    return [pl.BlockSpec(memory_space=pltpu.VMEM)] * count


def local(populations, solid_mask, displacement, stiffness, neighbours, owners, stencil_base, stencil_weights):
    def f32(*shape):
        return jax.ShapeDtypeStruct(shape, F32)

    def vmem(*shape):
        return pltpu.VMEM(shape, F32)

    halo = (2, 5, SY, SZ), (2, 5, SX, SZ), (2, 8, 128)
    shifted, body = pl.pallas_call(
        gather_kernel,
        out_shape=(f32(19, SX, SY, SZ), f32(3, SX, SY, SZ)),
        in_specs=[pl.BlockSpec(memory_space=pltpu.HBM)] * 7,
        out_specs=tuple(whole(2)),
        scratch_shapes=[
            vmem(19, SX, SY, SZ), vmem(3, 1024), vmem(1, 1024), pltpu.VMEM((6, 1024), I32), pltpu.VMEM((1, 1024), I32),
            pltpu.VMEM((1, 1024), I32), vmem(12, 1024), vmem(4, 8, 1024), vmem(GROUP, 4, 128), vmem(GROUP, 4, 128),
            *(vmem(*shape) for shape in halo), *(vmem(*shape) for shape in halo),
            vmem(4, 8, SZ), vmem(4, SY, SZ), vmem(4, SX, SZ),
            vmem(16, 4, 4, 128), pltpu.VMEM((384, 256), BF16), pltpu.VMEM((256, 256), BF16), vmem(384, 256),
            pltpu.SemaphoreType.DMA((7,)),
            pltpu.SemaphoreType.DMA((GROUP,)),
            pltpu.SemaphoreType.DMA((GROUP,)),
            pltpu.SemaphoreType.DMA((18,)),
            pltpu.SemaphoreType.DMA((18,)),
            pltpu.SemaphoreType.REGULAR((GROUP,)),
            pltpu.SemaphoreType.REGULAR((N_GZ,)),
        ],
        compiler_params=pltpu.CompilerParams(
            collective_id=0, has_side_effects=True, vmem_limit_bytes=16 * 1024 * 1024
        ),
        name="gather",
    )(
        *(pltpu.with_memory_space_constraint(v, pltpu.HBM) for v in (
        populations, displacement, stiffness.reshape(1, 1024), neighbours,
        owners.reshape(1, 1024), stencil_base.reshape(1, 1024), stencil_weights))
    )
    return tuple(
        pl.pallas_call(
            collide_kernel,
            out_shape=(f32(19, SX, SY, SZ), f32(3, SX, SY, SZ)),
            in_specs=whole(3),
            out_specs=(pl.BlockSpec(memory_space=pltpu.HBM),) * 2,
            scratch_shapes=[vmem(19, SX, SY, SZ), pltpu.SemaphoreType.DMA((SX + 1,))],
            compiler_params=pltpu.CompilerParams(vmem_limit_bytes=8 * 1024 * 1024),
            name="collide",
        )(shifted, solid_mask, body)
    )


def solution(mesh):
    placed = (
        P(None, "gx", "gy", "gz"),
        P("gx", "gy", "gz"),
        P(None, ("gx", "gy", "gz")),
        P(("gx", "gy", "gz")),
        P(None, ("gx", "gy", "gz")),
        P(("gx", "gy", "gz"), None),
        P(("gx", "gy", "gz")),
        P(None, ("gx", "gy", "gz")),
    )
    return jax.shard_map(
        local,
        mesh=mesh,
        in_specs=placed,
        out_specs=(P(None, "gx", "gy", "gz"), P(None, "gx", "gy", "gz")),
        check_vma=False,
    )
```
